32 devices in a mesh: section: 4 (over y, x), band: 4 (over z), members: 2 (over core).
Axes of the slice: x: 2, y: 2, z: 4, core: 2. Of those that a mesh axis runs over, the one named last changes fastest.
Arguments:
- fields: bfloat16 [8, 16, 576, 128], P(('members', 'section'), 'band'), parts along dimension 0, may hold values from -6 to 6
- lat_taps: bfloat16 [2, 9, 128], replicated, may hold values from -1.5 to 1.5
- lon_taps: bfloat16 [2, 9, 128], replicated, may hold values from -1.5 to 1.5
- gains: float32 [2, 128], replicated, may hold values from 0.1 to 1.9
- w_in: bfloat16 [2, 128, 256], replicated, may hold values from -0.5 to 0.5
- w_out: bfloat16 [2, 256, 128], replicated, may hold values from -0.375 to 0.375
Outputs:
- final_states: bfloat16 [8, 16, 576, 128], P(('members', 'section'), 'band'), parts along dimension 0
The draws below stay inside these ranges and needn't reach their ends.
There are 2 independent parts, one for each index of `members`. The reference program is written for one: setup_inputs(seed, part) draws one part's arguments, and reference() takes and returns one part's arrays. A program takes and returns all parts, laid end to end along the dimension named above; an argument that names none is the same for every part. Nothing has to cross between parts.
All inputs are finite; a program needn't handle non-finite values.
Results may differ from the reference program's by a relative error of at most 0.0063.
Values may be sent and summed in bfloat16 or wider, within the bound.
No kernel may reach another device: no remote copies, remote signals or barrier semaphores. Data moves between devices by JAX's collectives and lax.ppermute only.
A program may use at most 64 MiB of HBM per device.

```python
import jax
import jax.numpy as jnp
from jax import lax

C = 128
H = 256
LON = 576
DLON = 3
LAYERS = 2
MB = 4
LAT = 16


def shard_levels(rng, dims, split, low, largest):
    def one(axis_at, shards_of):
        heights = jax.random.uniform(jax.random.fold_in(jax.random.fold_in(rng, 6), axis_at), (shards_of,), jnp.float32, low / len(split), largest / len(split))
        return jnp.repeat(jnp.exp(heights), dims[axis_at] // shards_of).reshape((-1,) + (1,) * (len(dims) - axis_at - 1))

    factor_of = one(*split[0])
    for cut in split[1:]:
        factor_of = factor_of * one(*cut)
    return factor_of


def normal_values(rng, dims, deviation, most, split=(), dtype=jnp.bfloat16):
    level = shard_levels(rng, dims, split, -0.22, 0.18) if split else 1.0
    entries = jax.random.normal(rng, dims, jnp.float32) * deviation * level
    return jnp.minimum(jnp.maximum(entries, -most), most).astype(dtype)


def setup_inputs(seed: int = 0, part: int = 0) -> dict:
    key_of = jax.random.split(jax.random.key(seed), 7)
    part_splits = jax.random.split(jax.random.fold_in(key_of[6], part), 7)
    fields = normal_values(part_splits[0], (MB, LAT, LON, C), 1.0, 6.0, ((0, 4), (1, 4)))
    lat_taps = normal_values(key_of[1], (LAYERS, 9, C), 0.33, 1.5)
    lon_taps = normal_values(key_of[2], (LAYERS, 9, C), 0.33, 1.5)
    gains = jnp.clip(1.0 + 0.18 * jax.random.normal(key_of[3], (LAYERS, C), jnp.float32), 0.1, 1.9)
    w_in = normal_values(key_of[4], (LAYERS, C, H), C ** -0.5, 0.5)
    w_out = normal_values(key_of[5], (LAYERS, H, C), H ** -0.5, 0.375)
    return dict(fields=fields, lat_taps=lat_taps, lon_taps=lon_taps, gains=gains, w_in=w_in, w_out=w_out)


def layer_step(state, lat_w, lon_w, gain, proj_in, proj_out):
    rows = state.shape[0]
    wide = state.astype(jnp.float32)
    padded = jnp.pad(wide, ((4, 4), (0, 0), (0, 0)))
    lat_tap = lat_w.astype(jnp.float32)
    latmix = jnp.zeros_like(wide)
    for k in range(9):
        latmix = latmix + padded[k:k + rows] * lat_tap[k]
    latmix = latmix.astype(jnp.bfloat16).astype(jnp.float32)
    lon_tap = lon_w.astype(jnp.float32)
    lonmix = jnp.zeros_like(wide)
    for k in range(9):
        lonmix = lonmix + jnp.roll(latmix, -DLON * (k - 4), axis=1) * lon_tap[k]
    mean = lax.optimization_barrier(jnp.mean(lonmix, axis=-1, keepdims=True))
    centred = lonmix - mean
    var = lax.optimization_barrier(jnp.mean(centred * centred, axis=-1, keepdims=True))
    normed = (centred / jnp.sqrt(var + 1e-06) * gain).astype(jnp.bfloat16)
    flat = normed.reshape(-1, normed.shape[-1])
    hidden = jax.nn.gelu(jnp.dot(flat, proj_in, preferred_element_type=jnp.float32), approximate=False).astype(jnp.bfloat16)
    delta = jnp.dot(hidden, proj_out, preferred_element_type=jnp.float32).reshape(wide.shape)
    return (wide + delta).astype(jnp.bfloat16)

def reference(fields, lat_taps, lon_taps, gains, w_in, w_out):

    def run(state):
        for layer in range(LAYERS):
            state = layer_step(state, lat_taps[layer], lon_taps[layer], gains[layer], w_in[layer], w_out[layer])
        return state
    return lax.map(run, fields)
```

```python
import functools

import jax
import jax.numpy as jnp
from jax import lax
from jax.experimental import pallas as pl
from jax.experimental.pallas import tpu as pltpu
from jax.sharding import PartitionSpec as P

DLON = 3
LAYERS = 2
TAPS = 9
REACH = TAPS // 2
PAD = 16
CHUNKS = 1
TILE = 32


def gelu(x):
    return 0.5 * x * (1.0 + lax.erf(x * 0.7071067811865476))


def chunk_kernel(first, last, width, *refs):
    refs = list(refs)
    lat_w, lon_w, gain, w_in, w_out, own, above, below = refs[:8]
    refs = refs[8:]
    if not first:
        prev_own, prev_mix = refs[:2]
        refs = refs[2:]
    if last and not first:
        first_own, first_mix = refs[:2]
        refs = refs[2:]
    out = refs.pop(0)
    if not last:
        tail = refs.pop(0)
    if first and not last:
        head = refs.pop(0)
    mix, state = refs
    rows = own.shape[0]
    channels = own.shape[2]
    start = 0 if first else 2 * PAD

    if not first:
        mix[:, : 2 * PAD] = prev_mix[...].astype(jnp.float32)
        state[:, : 2 * PAD] = prev_own[:, prev_own.shape[1] - 2 * PAD :]
    if last and not first:
        mix[:, start + width :] = first_mix[...].astype(jnp.float32)
        state[:, start + width :] = first_own[:, : 2 * PAD]

    lat_tap = [jnp.broadcast_to(lat_w[k : k + 1], (PAD, channels)) for k in range(TAPS)]

    def mix_tile(t, carry):
        at = pl.multiple_of(t * PAD, PAD)
        to = pl.multiple_of(start + t * PAD, PAD)
        strip = [above[r, pl.ds(at, PAD)] for r in range(REACH)]
        mine = [own[r, pl.ds(at, PAD)] for r in range(rows)]
        strip = strip + mine + [below[r, pl.ds(at, PAD)] for r in range(REACH)]
        strip = [s.astype(jnp.float32) for s in strip]
        for r in range(rows):
            total = strip[r] * lat_tap[0]
            for k in range(1, TAPS):
                total = total + strip[r + k] * lat_tap[k]
            mix[r, pl.ds(to, PAD)] = total.astype(jnp.bfloat16).astype(jnp.float32)
            state[r, pl.ds(to, PAD)] = mine[r]
        return carry

    lax.fori_loop(0, width // PAD, mix_tile, 0)

    if not last:
        tail[...] = mix[:, start + width - 2 * PAD : start + width].astype(jnp.bfloat16)
    if first and not last:
        head[...] = mix[:, : 2 * PAD].astype(jnp.bfloat16)
    if first and last:
        mix[:, width:] = mix[:, : 2 * PAD]
        state[:, width:] = state[:, : 2 * PAD]

    lon_tap = [lon_w[k : k + 1] for k in range(TAPS)]
    scale = gain[...]
    made = out.shape[1]

    def rest(at, tile):
        parts = []
        for r in range(rows):
            lon = mix[r, pl.ds(at + PAD - DLON * REACH, tile)] * lon_tap[0]
            for k in range(1, TAPS):
                lon = lon + mix[r, pl.ds(at + PAD + DLON * (k - REACH), tile)] * lon_tap[k]
            parts.append(lon)
        lon = jnp.concatenate(parts, axis=0)
        mean = jnp.mean(lon, axis=-1, keepdims=True)
        centred = lon - mean
        var = jnp.mean(centred * centred, axis=-1, keepdims=True)
        normed = (centred * lax.rsqrt(var + 1e-06) * scale).astype(jnp.bfloat16)
        hidden = jnp.dot(normed, w_in[...], preferred_element_type=jnp.float32)
        hidden = gelu(hidden).astype(jnp.bfloat16)
        delta = jnp.dot(hidden, w_out[...], preferred_element_type=jnp.float32)
        for r in range(rows):
            new = state[r, pl.ds(at + PAD, tile)].astype(jnp.float32) + delta[r * tile : (r + 1) * tile]
            out[r, pl.ds(at, tile)] = new.astype(jnp.bfloat16)

    for at in range(0, made, TILE):
        rest(at, min(TILE, made - at))


def layer_chunk(weights, chunk, prev, first_chunk, first, last):
    own, above, below = chunk
    rows, width, channels = own.shape
    made = width + (0 if first else PAD) + (0 if last else -PAD) + (PAD if last else 0) - (PAD if first else 0)
    window = made + 2 * PAD
    args = list(weights) + [own, above, below]
    if not first:
        args += list(prev)
    if last and not first:
        args += list(first_chunk)
    strip = jax.ShapeDtypeStruct((rows, 2 * PAD, channels), jnp.bfloat16)
    outs = [jax.ShapeDtypeStruct((rows, made, channels), jnp.bfloat16)]
    if not last:
        outs.append(strip)
    if first and not last:
        outs.append(strip)
    cells = rows * made
    hidden = weights[3].shape[1]
    return pl.pallas_call(
        functools.partial(chunk_kernel, first, last, width),
        out_shape=outs,
        in_specs=[pl.BlockSpec(memory_space=pltpu.VMEM)] * len(args),
        out_specs=[pl.BlockSpec(memory_space=pltpu.VMEM)] * len(outs),
        scratch_shapes=[
            pltpu.VMEM((rows, window, channels), jnp.float32),
            pltpu.VMEM((rows, window, channels), jnp.bfloat16),
        ],
        compiler_params=pltpu.CompilerParams(vmem_limit_bytes=24 * 2**20),
        cost_estimate=pl.CostEstimate(
            flops=4 * cells * channels * hidden, bytes_accessed=8 * cells * channels, transcendentals=cells * hidden
        ),
    )(*args)


def splits(total):
    tiles = total // PAD
    edges = [PAD * ((tiles * c) // CHUNKS) for c in range(CHUNKS)] + [total]
    return [(lo, hi) for lo, hi in zip(edges[:-1], edges[1:])]


def member_step(state, weights, bands):
    rows, lons, _ = state.shape
    up = [(b, b + 1) for b in range(bands - 1)]
    down = [(b + 1, b) for b in range(bands - 1)]
    chunks = [state[:, lo:hi] for lo, hi in splits(lons)]
    for layer in range(LAYERS):
        halos = [
            (lax.ppermute(own[rows - REACH :], "band", up), lax.ppermute(own[:REACH], "band", down))
            for own in chunks
        ]
        made, prev, first_chunk = [], None, None
        for c, own in enumerate(chunks):
            first, last = c == 0, c == len(chunks) - 1
            got = layer_chunk(weights[layer], (own,) + halos[c], prev, first_chunk, first, last)
            made.append(got[0])
            if not last:
                prev = (own, got[1])
            if first and not last:
                first_chunk = (own[:, : 2 * PAD], got[2])
        chunks = made
    whole = jnp.concatenate(chunks, axis=1)
    return jnp.roll(whole, LAYERS * PAD, axis=1)


def solution(mesh):
    bands = mesh.shape["band"]

    def shards(fields, lat_taps, lon_taps, gains, w_in, w_out):
        weights = [
            (
                lat_taps[layer].astype(jnp.float32),
                lon_taps[layer].astype(jnp.float32),
                gains[layer : layer + 1],
                w_in[layer],
                w_out[layer],
            )
            for layer in range(LAYERS)
        ]
        return jnp.stack([member_step(fields[m], weights, bands) for m in range(fields.shape[0])])

    return jax.shard_map(
        shards,
        mesh=mesh,
        in_specs=(P(("members", "section"), "band", None, None), P(), P(), P(), P(), P()),
        out_specs=P(("members", "section"), "band", None, None),
        check_vma=False,
    )
```

```python
import functools

import jax
import jax.numpy as jnp
from jax import lax
from jax.experimental import pallas as pl
from jax.experimental.pallas import tpu as pltpu
from jax.sharding import PartitionSpec as P

DLON = 3
LAYERS = 2
TAPS = 9
REACH = TAPS // 2
PAD = 16
CHUNKS = 4
TILE = 32


def gelu(x):
    return 0.5 * x * (1.0 + lax.erf(x * 0.7071067811865476))


def chunk_kernel(first, last, width, *refs):
    refs = list(refs)
    lat_w, lon_w, gain, w_in, w_out, own, above, below = refs[:8]
    refs = refs[8:]
    if not first:
        prev_own, prev_mix = refs[:2]
        refs = refs[2:]
    if last and not first:
        first_own, first_mix = refs[:2]
        refs = refs[2:]
    out = refs.pop(0)
    if not last:
        tail = refs.pop(0)
    if first and not last:
        head = refs.pop(0)
    mix, state = refs
    rows = own.shape[0]
    channels = own.shape[2]
    start = 0 if first else 2 * PAD

    if not first:
        mix[:, : 2 * PAD] = prev_mix[...].astype(jnp.float32)
        state[:, : 2 * PAD] = prev_own[:, prev_own.shape[1] - 2 * PAD :]
    if last and not first:
        mix[:, start + width :] = first_mix[...].astype(jnp.float32)
        state[:, start + width :] = first_own[:, : 2 * PAD]

    lat_tap = [jnp.broadcast_to(lat_w[k : k + 1], (PAD, channels)) for k in range(TAPS)]

    def mix_tile(t, carry):
        at = pl.multiple_of(t * PAD, PAD)
        to = pl.multiple_of(start + t * PAD, PAD)
        strip = [above[r, pl.ds(at, PAD)] for r in range(REACH)]
        mine = [own[r, pl.ds(at, PAD)] for r in range(rows)]
        strip = strip + mine + [below[r, pl.ds(at, PAD)] for r in range(REACH)]
        strip = [s.astype(jnp.float32) for s in strip]
        for r in range(rows):
            total = strip[r] * lat_tap[0]
            for k in range(1, TAPS):
                total = total + strip[r + k] * lat_tap[k]
            mix[r, pl.ds(to, PAD)] = total.astype(jnp.bfloat16).astype(jnp.float32)
            state[r, pl.ds(to, PAD)] = mine[r]
        return carry

    lax.fori_loop(0, width // PAD, mix_tile, 0)

    if not last:
        tail[...] = mix[:, start + width - 2 * PAD : start + width].astype(jnp.bfloat16)
    if first and not last:
        head[...] = mix[:, : 2 * PAD].astype(jnp.bfloat16)
    if first and last:
        mix[:, width:] = mix[:, : 2 * PAD]
        state[:, width:] = state[:, : 2 * PAD]

    lon_tap = [lon_w[k : k + 1] for k in range(TAPS)]
    scale = gain[...]
    made = out.shape[1]

    def rest(at, tile):
        parts = []
        for r in range(rows):
            lon = mix[r, pl.ds(at + PAD - DLON * REACH, tile)] * lon_tap[0]
            for k in range(1, TAPS):
                lon = lon + mix[r, pl.ds(at + PAD + DLON * (k - REACH), tile)] * lon_tap[k]
            parts.append(lon)
        lon = jnp.concatenate(parts, axis=0)
        mean = jnp.mean(lon, axis=-1, keepdims=True)
        centred = lon - mean
        var = jnp.mean(centred * centred, axis=-1, keepdims=True)
        normed = (centred * lax.rsqrt(var + 1e-06) * scale).astype(jnp.bfloat16)
        hidden = jnp.dot(normed, w_in[...], preferred_element_type=jnp.float32)
        hidden = gelu(hidden).astype(jnp.bfloat16)
        delta = jnp.dot(hidden, w_out[...], preferred_element_type=jnp.float32)
        for r in range(rows):
            new = state[r, pl.ds(at + PAD, tile)].astype(jnp.float32) + delta[r * tile : (r + 1) * tile]
            out[r, pl.ds(at, tile)] = new.astype(jnp.bfloat16)

    for at in range(0, made, TILE):
        rest(at, min(TILE, made - at))


def layer_chunk(weights, chunk, prev, first_chunk, first, last):
    own, above, below = chunk
    rows, width, channels = own.shape
    made = width + (0 if first else PAD) + (0 if last else -PAD) + (PAD if last else 0) - (PAD if first else 0)
    window = made + 2 * PAD
    args = list(weights) + [own, above, below]
    if not first:
        args += list(prev)
    if last and not first:
        args += list(first_chunk)
    strip = jax.ShapeDtypeStruct((rows, 2 * PAD, channels), jnp.bfloat16)
    outs = [jax.ShapeDtypeStruct((rows, made, channels), jnp.bfloat16)]
    if not last:
        outs.append(strip)
    if first and not last:
        outs.append(strip)
    cells = rows * made
    hidden = weights[3].shape[1]
    return pl.pallas_call(
        functools.partial(chunk_kernel, first, last, width),
        out_shape=outs,
        in_specs=[pl.BlockSpec(memory_space=pltpu.VMEM)] * len(args),
        out_specs=[pl.BlockSpec(memory_space=pltpu.VMEM)] * len(outs),
        scratch_shapes=[
            pltpu.VMEM((rows, window, channels), jnp.float32),
            pltpu.VMEM((rows, window, channels), jnp.bfloat16),
        ],
        compiler_params=pltpu.CompilerParams(vmem_limit_bytes=24 * 2**20),
        cost_estimate=pl.CostEstimate(
            flops=4 * cells * channels * hidden, bytes_accessed=8 * cells * channels, transcendentals=cells * hidden
        ),
    )(*args)


def splits(total):
    tiles = total // PAD
    edges = [PAD * ((tiles * c) // CHUNKS) for c in range(CHUNKS)] + [total]
    return [(lo, hi) for lo, hi in zip(edges[:-1], edges[1:])]


def member_step(state, weights, bands):
    rows, lons, _ = state.shape
    up = [(b, b + 1) for b in range(bands - 1)]
    down = [(b + 1, b) for b in range(bands - 1)]
    chunks = [state[:, lo:hi] for lo, hi in splits(lons)]
    for layer in range(LAYERS):
        halos = [
            (lax.ppermute(own[rows - REACH :], "band", up), lax.ppermute(own[:REACH], "band", down))
            for own in chunks
        ]
        made, prev, first_chunk = [], None, None
        for c, own in enumerate(chunks):
            first, last = c == 0, c == len(chunks) - 1
            got = layer_chunk(weights[layer], (own,) + halos[c], prev, first_chunk, first, last)
            made.append(got[0])
            if not last:
                prev = (own, got[1])
            if first and not last:
                first_chunk = (own[:, : 2 * PAD], got[2])
        chunks = made
    whole = jnp.concatenate(chunks, axis=1)
    return jnp.roll(whole, LAYERS * PAD, axis=1)


def solution(mesh):
    bands = mesh.shape["band"]

    def shards(fields, lat_taps, lon_taps, gains, w_in, w_out):
        weights = [
            (
                lat_taps[layer].astype(jnp.float32),
                lon_taps[layer].astype(jnp.float32),
                gains[layer : layer + 1],
                w_in[layer],
                w_out[layer],
            )
            for layer in range(LAYERS)
        ]
        return jnp.stack([member_step(fields[m], weights, bands) for m in range(fields.shape[0])])

    return jax.shard_map(
        shards,
        mesh=mesh,
        in_specs=(P(("members", "section"), "band", None, None), P(), P(), P(), P(), P()),
        out_specs=P(("members", "section"), "band", None, None),
        check_vma=False,
    )
```

```python
import functools

import jax
import jax.numpy as jnp
from jax import lax
from jax.experimental import pallas as pl
from jax.experimental.pallas import tpu as pltpu
from jax.sharding import PartitionSpec as P

DLON = 3
LAYERS = 2
TAPS = 9
REACH = TAPS // 2
PAD = 16
CHUNKS = 1
TILE = 32


def gelu(x):
    return 0.5 * x * (1.0 + lax.erf(x * 0.7071067811865476))


def chunk_kernel(bands, first, last, width, *refs):
    refs = list(refs)
    lat_w, lon_w, gain, w_in, w_out, own, even_swap, odd_swap = refs[:8]
    refs = refs[8:]
    if not first:
        prev_own, prev_mix = refs[:2]
        refs = refs[2:]
    if last and not first:
        first_own, first_mix = refs[:2]
        refs = refs[2:]
    out = refs.pop(0)
    if not last:
        tail = refs.pop(0)
    if first and not last:
        head = refs.pop(0)
    mix, state = refs
    rows = own.shape[0]
    channels = own.shape[2]
    start = 0 if first else 2 * PAD

    if not first:
        mix[:, : 2 * PAD] = prev_mix[...].astype(jnp.float32)
        state[:, : 2 * PAD] = prev_own[:, prev_own.shape[1] - 2 * PAD :]
    if last and not first:
        mix[:, start + width :] = first_mix[...].astype(jnp.float32)
        state[:, start + width :] = first_own[:, : 2 * PAD]

    band = lax.axis_index("band")
    is_odd = lax.rem(band, 2) == 1
    top, bottom = band == 0, band == bands - 1
    lat_tap = [jnp.broadcast_to(lat_w[k : k + 1], (PAD, channels)) for k in range(TAPS)]

    def mix_tile(t, carry):
        at = pl.multiple_of(t * PAD, PAD)
        to = pl.multiple_of(start + t * PAD, PAD)
        evens = [even_swap[r, pl.ds(at, PAD)] for r in range(REACH)]
        odds = [odd_swap[r, pl.ds(at, PAD)] for r in range(REACH)]
        none = jnp.zeros_like(evens[0])
        above = [jnp.where(top, none, jnp.where(is_odd, e, o)) for e, o in zip(evens, odds)]
        below = [jnp.where(bottom, none, jnp.where(is_odd, o, e)) for e, o in zip(evens, odds)]
        mine = [own[r, pl.ds(at, PAD)] for r in range(rows)]
        strip = [s.astype(jnp.float32) for s in above + mine + below]
        for r in range(rows):
            total = strip[r] * lat_tap[0]
            for k in range(1, TAPS):
                total = total + strip[r + k] * lat_tap[k]
            mix[r, pl.ds(to, PAD)] = total.astype(jnp.bfloat16).astype(jnp.float32)
            state[r, pl.ds(to, PAD)] = mine[r]
        return carry

    lax.fori_loop(0, width // PAD, mix_tile, 0)

    if not last:
        tail[...] = mix[:, start + width - 2 * PAD : start + width].astype(jnp.bfloat16)
    if first and not last:
        head[...] = mix[:, : 2 * PAD].astype(jnp.bfloat16)
    if first and last:
        mix[:, width:] = mix[:, : 2 * PAD]
        state[:, width:] = state[:, : 2 * PAD]

    lon_tap = [lon_w[k : k + 1] for k in range(TAPS)]
    scale = gain[...]
    made = out.shape[1]

    def rest(at, tile):
        parts = []
        for r in range(rows):
            lon = mix[r, pl.ds(at + PAD - DLON * REACH, tile)] * lon_tap[0]
            for k in range(1, TAPS):
                lon = lon + mix[r, pl.ds(at + PAD + DLON * (k - REACH), tile)] * lon_tap[k]
            parts.append(lon)
        lon = jnp.concatenate(parts, axis=0)
        mean = jnp.mean(lon, axis=-1, keepdims=True)
        centred = lon - mean
        var = jnp.mean(centred * centred, axis=-1, keepdims=True)
        normed = (centred * lax.rsqrt(var + 1e-06) * scale).astype(jnp.bfloat16)
        hidden = jnp.dot(normed, w_in[...], preferred_element_type=jnp.float32)
        hidden = gelu(hidden).astype(jnp.bfloat16)
        delta = jnp.dot(hidden, w_out[...], preferred_element_type=jnp.float32)
        for r in range(rows):
            new = state[r, pl.ds(at + PAD, tile)].astype(jnp.float32) + delta[r * tile : (r + 1) * tile]
            out[r, pl.ds(at, tile)] = new.astype(jnp.bfloat16)

    for at in range(0, made, TILE):
        rest(at, min(TILE, made - at))


def layer_chunk(bands, weights, chunk, prev, first_chunk, first, last):
    own, even_swap, odd_swap = chunk
    rows, width, channels = own.shape
    made = width + (0 if first else PAD) + (0 if last else -PAD) + (PAD if last else 0) - (PAD if first else 0)
    window = made + 2 * PAD
    args = list(weights) + [own, even_swap, odd_swap]
    if not first:
        args += list(prev)
    if last and not first:
        args += list(first_chunk)
    strip = jax.ShapeDtypeStruct((rows, 2 * PAD, channels), jnp.bfloat16)
    outs = [jax.ShapeDtypeStruct((rows, made, channels), jnp.bfloat16)]
    if not last:
        outs.append(strip)
    if first and not last:
        outs.append(strip)
    cells = rows * made
    hidden = weights[3].shape[1]
    return pl.pallas_call(
        functools.partial(chunk_kernel, bands, first, last, width),
        out_shape=outs,
        in_specs=[pl.BlockSpec(memory_space=pltpu.VMEM)] * len(args),
        out_specs=[pl.BlockSpec(memory_space=pltpu.VMEM)] * len(outs),
        scratch_shapes=[
            pltpu.VMEM((rows, window, channels), jnp.float32),
            pltpu.VMEM((rows, window, channels), jnp.bfloat16),
        ],
        compiler_params=pltpu.CompilerParams(vmem_limit_bytes=24 * 2**20),
        cost_estimate=pl.CostEstimate(
            flops=4 * cells * channels * hidden, bytes_accessed=8 * cells * channels, transcendentals=cells * hidden
        ),
    )(*args)


def splits(total):
    tiles = total // PAD
    edges = [PAD * ((tiles * c) // CHUNKS) for c in range(CHUNKS)] + [total]
    return [(lo, hi) for lo, hi in zip(edges[:-1], edges[1:])]


def swaps(bands, start):
    to = list(range(bands))
    for b in range(start, bands - 1, 2):
        to[b], to[b + 1] = b + 1, b
    return list(enumerate(to))


def member_step(state, weights, bands):
    rows, lons, _ = state.shape
    even_pairs, odd_pairs = swaps(bands, 0), swaps(bands, 1)
    assert rows == REACH
    chunks = [state[:, lo:hi] for lo, hi in splits(lons)]
    for layer in range(LAYERS):
        halos = [(lax.ppermute(own, "band", even_pairs), lax.ppermute(own, "band", odd_pairs)) for own in chunks]
        made, prev, first_chunk = [], None, None
        for c, own in enumerate(chunks):
            first, last = c == 0, c == len(chunks) - 1
            got = layer_chunk(bands, weights[layer], (own,) + halos[c], prev, first_chunk, first, last)
            made.append(got[0])
            if not last:
                prev = (own, got[1])
            if first and not last:
                first_chunk = (own[:, : 2 * PAD], got[2])
        chunks = made
    whole = jnp.concatenate(chunks, axis=1)
    return jnp.roll(whole, LAYERS * PAD, axis=1)


def solution(mesh):
    bands = mesh.shape["band"]

    def shards(fields, lat_taps, lon_taps, gains, w_in, w_out):
        weights = [
            (
                lat_taps[layer].astype(jnp.float32),
                lon_taps[layer].astype(jnp.float32),
                gains[layer : layer + 1],
                w_in[layer],
                w_out[layer],
            )
            for layer in range(LAYERS)
        ]
        return jnp.stack([member_step(fields[m], weights, bands) for m in range(fields.shape[0])])

    return jax.shard_map(
        shards,
        mesh=mesh,
        in_specs=(P(("members", "section"), "band", None, None), P(), P(), P(), P(), P()),
        out_specs=P(("members", "section"), "band", None, None),
        check_vma=False,
    )
```

```python
import functools

import jax
import jax.numpy as jnp
from jax import lax
from jax.experimental import pallas as pl
from jax.experimental.pallas import tpu as pltpu
from jax.sharding import PartitionSpec as P

DLON = 3
LAYERS = 2
TAPS = 9
REACH = TAPS // 2
PAD = 16
CHUNKS = 2
TILE = 32


def gelu(x):
    return 0.5 * x * (1.0 + lax.erf(x * 0.7071067811865476))


def chunk_kernel(bands, first, last, width, *refs):
    refs = list(refs)
    lat_w, lon_w, gain, w_in, w_out, own, even_swap, odd_swap = refs[:8]
    refs = refs[8:]
    if not first:
        prev_own, prev_mix = refs[:2]
        refs = refs[2:]
    if last and not first:
        first_own, first_mix = refs[:2]
        refs = refs[2:]
    out = refs.pop(0)
    if not last:
        tail = refs.pop(0)
    if first and not last:
        head = refs.pop(0)
    mix, state = refs
    rows = own.shape[0]
    channels = own.shape[2]
    start = 0 if first else 2 * PAD

    if not first:
        mix[:, : 2 * PAD] = prev_mix[...].astype(jnp.float32)
        state[:, : 2 * PAD] = prev_own[:, prev_own.shape[1] - 2 * PAD :]
    if last and not first:
        mix[:, start + width :] = first_mix[...].astype(jnp.float32)
        state[:, start + width :] = first_own[:, : 2 * PAD]

    band = lax.axis_index("band")
    is_odd = lax.rem(band, 2) == 1
    top, bottom = band == 0, band == bands - 1
    lat_tap = [jnp.broadcast_to(lat_w[k : k + 1], (PAD, channels)) for k in range(TAPS)]

    def mix_tile(t, carry):
        at = pl.multiple_of(t * PAD, PAD)
        to = pl.multiple_of(start + t * PAD, PAD)
        evens = [even_swap[r, pl.ds(at, PAD)] for r in range(REACH)]
        odds = [odd_swap[r, pl.ds(at, PAD)] for r in range(REACH)]
        none = jnp.zeros_like(evens[0])
        above = [jnp.where(top, none, jnp.where(is_odd, e, o)) for e, o in zip(evens, odds)]
        below = [jnp.where(bottom, none, jnp.where(is_odd, o, e)) for e, o in zip(evens, odds)]
        mine = [own[r, pl.ds(at, PAD)] for r in range(rows)]
        strip = [s.astype(jnp.float32) for s in above + mine + below]
        for r in range(rows):
            total = strip[r] * lat_tap[0]
            for k in range(1, TAPS):
                total = total + strip[r + k] * lat_tap[k]
            mix[r, pl.ds(to, PAD)] = total.astype(jnp.bfloat16).astype(jnp.float32)
            state[r, pl.ds(to, PAD)] = mine[r]
        return carry

    lax.fori_loop(0, width // PAD, mix_tile, 0)

    if not last:
        tail[...] = mix[:, start + width - 2 * PAD : start + width].astype(jnp.bfloat16)
    if first and not last:
        head[...] = mix[:, : 2 * PAD].astype(jnp.bfloat16)
    if first and last:
        mix[:, width:] = mix[:, : 2 * PAD]
        state[:, width:] = state[:, : 2 * PAD]

    lon_tap = [lon_w[k : k + 1] for k in range(TAPS)]
    scale = gain[...]
    made = out.shape[1]

    def rest(at, tile):
        parts = []
        for r in range(rows):
            lon = mix[r, pl.ds(at + PAD - DLON * REACH, tile)] * lon_tap[0]
            for k in range(1, TAPS):
                lon = lon + mix[r, pl.ds(at + PAD + DLON * (k - REACH), tile)] * lon_tap[k]
            parts.append(lon)
        lon = jnp.concatenate(parts, axis=0)
        mean = jnp.mean(lon, axis=-1, keepdims=True)
        centred = lon - mean
        var = jnp.mean(centred * centred, axis=-1, keepdims=True)
        normed = (centred * lax.rsqrt(var + 1e-06) * scale).astype(jnp.bfloat16)
        hidden = jnp.dot(normed, w_in[...], preferred_element_type=jnp.float32)
        hidden = gelu(hidden).astype(jnp.bfloat16)
        delta = jnp.dot(hidden, w_out[...], preferred_element_type=jnp.float32)
        for r in range(rows):
            new = state[r, pl.ds(at + PAD, tile)].astype(jnp.float32) + delta[r * tile : (r + 1) * tile]
            out[r, pl.ds(at, tile)] = new.astype(jnp.bfloat16)

    for at in range(0, made, TILE):
        rest(at, min(TILE, made - at))


def layer_chunk(bands, weights, chunk, prev, first_chunk, first, last):
    own, even_swap, odd_swap = chunk
    rows, width, channels = own.shape
    made = width + (0 if first else PAD) + (0 if last else -PAD) + (PAD if last else 0) - (PAD if first else 0)
    window = made + 2 * PAD
    args = list(weights) + [own, even_swap, odd_swap]
    if not first:
        args += list(prev)
    if last and not first:
        args += list(first_chunk)
    strip = jax.ShapeDtypeStruct((rows, 2 * PAD, channels), jnp.bfloat16)
    outs = [jax.ShapeDtypeStruct((rows, made, channels), jnp.bfloat16)]
    if not last:
        outs.append(strip)
    if first and not last:
        outs.append(strip)
    cells = rows * made
    hidden = weights[3].shape[1]
    return pl.pallas_call(
        functools.partial(chunk_kernel, bands, first, last, width),
        out_shape=outs,
        in_specs=[pl.BlockSpec(memory_space=pltpu.VMEM)] * len(args),
        out_specs=[pl.BlockSpec(memory_space=pltpu.VMEM)] * len(outs),
        scratch_shapes=[
            pltpu.VMEM((rows, window, channels), jnp.float32),
            pltpu.VMEM((rows, window, channels), jnp.bfloat16),
        ],
        compiler_params=pltpu.CompilerParams(vmem_limit_bytes=24 * 2**20),
        cost_estimate=pl.CostEstimate(
            flops=4 * cells * channels * hidden, bytes_accessed=8 * cells * channels, transcendentals=cells * hidden
        ),
    )(*args)


def splits(total):
    tiles = total // PAD
    edges = [PAD * ((tiles * c) // CHUNKS) for c in range(CHUNKS)] + [total]
    return [(lo, hi) for lo, hi in zip(edges[:-1], edges[1:])]


def swaps(bands, start):
    to = list(range(bands))
    for b in range(start, bands - 1, 2):
        to[b], to[b + 1] = b + 1, b
    return list(enumerate(to))


def member_step(state, weights, bands):
    rows, lons, _ = state.shape
    even_pairs, odd_pairs = swaps(bands, 0), swaps(bands, 1)
    assert rows == REACH
    chunks = [state[:, lo:hi] for lo, hi in splits(lons)]
    for layer in range(LAYERS):
        halos = [(lax.ppermute(own, "band", even_pairs), lax.ppermute(own, "band", odd_pairs)) for own in chunks]
        made, prev, first_chunk = [], None, None
        for c, own in enumerate(chunks):
            first, last = c == 0, c == len(chunks) - 1
            got = layer_chunk(bands, weights[layer], (own,) + halos[c], prev, first_chunk, first, last)
            made.append(got[0])
            if not last:
                prev = (own, got[1])
            if first and not last:
                first_chunk = (own[:, : 2 * PAD], got[2])
        chunks = made
    whole = jnp.concatenate(chunks, axis=1)
    return jnp.roll(whole, LAYERS * PAD, axis=1)


def solution(mesh):
    bands = mesh.shape["band"]

    def shards(fields, lat_taps, lon_taps, gains, w_in, w_out):
        weights = [
            (
                lat_taps[layer].astype(jnp.float32),
                lon_taps[layer].astype(jnp.float32),
                gains[layer : layer + 1],
                w_in[layer],
                w_out[layer],
            )
            for layer in range(LAYERS)
        ]
        return jnp.stack([member_step(fields[m], weights, bands) for m in range(fields.shape[0])])

    return jax.shard_map(
        shards,
        mesh=mesh,
        in_specs=(P(("members", "section"), "band", None, None), P(), P(), P(), P(), P()),
        out_specs=P(("members", "section"), "band", None, None),
        check_vma=False,
    )
```

```python
import functools

import jax
import jax.numpy as jnp
from jax import lax
from jax.experimental import pallas as pl
from jax.experimental.pallas import tpu as pltpu
from jax.sharding import PartitionSpec as P

DLON = 3
LAYERS = 2
TAPS = 9
REACH = TAPS // 2
PAD = 16
TILE = 32


def gelu(x):
    return 0.5 * x * (1.0 + lax.erf(x * 0.7071067811865476))


def chunk_kernel(bands, first, last, width, *refs):
    refs = list(refs)
    lat_w, lon_w, gain, w_in, w_out, own, even_swap, odd_swap = refs[:8]
    refs = refs[8:]
    if not first:
        prev_own, prev_mix = refs[:2]
        refs = refs[2:]
    if last and not first:
        first_own, first_mix = refs[:2]
        refs = refs[2:]
    out = refs.pop(0)
    if not last:
        tail = refs.pop(0)
    if first and not last:
        head = refs.pop(0)
    mix, state = refs
    rows = own.shape[0]
    channels = own.shape[2]
    start = 0 if first else 2 * PAD

    if not first:
        mix[:, : 2 * PAD] = prev_mix[...].astype(jnp.float32)
        state[:, : 2 * PAD] = prev_own[:, prev_own.shape[1] - 2 * PAD :]
    if last and not first:
        mix[:, start + width :] = first_mix[...].astype(jnp.float32)
        state[:, start + width :] = first_own[:, : 2 * PAD]

    band = lax.axis_index("band")
    is_odd = lax.rem(band, 2) == 1
    top, bottom = band == 0, band == bands - 1
    lat_tap = [jnp.broadcast_to(lat_w[k : k + 1], (PAD, channels)) for k in range(TAPS)]

    def mix_tile(t, carry):
        at = pl.multiple_of(t * PAD, PAD)
        to = pl.multiple_of(start + t * PAD, PAD)
        evens = [even_swap[r, pl.ds(at, PAD)] for r in range(REACH)]
        odds = [odd_swap[r, pl.ds(at, PAD)] for r in range(REACH)]
        none = jnp.zeros_like(evens[0])
        above = [jnp.where(top, none, jnp.where(is_odd, e, o)) for e, o in zip(evens, odds)]
        below = [jnp.where(bottom, none, jnp.where(is_odd, o, e)) for e, o in zip(evens, odds)]
        mine = [own[r, pl.ds(at, PAD)] for r in range(rows)]
        strip = [s.astype(jnp.float32) for s in above + mine + below]
        for r in range(rows):
            total = strip[r] * lat_tap[0]
            for k in range(1, TAPS):
                total = total + strip[r + k] * lat_tap[k]
            mix[r, pl.ds(to, PAD)] = total.astype(jnp.bfloat16).astype(jnp.float32)
            state[r, pl.ds(to, PAD)] = mine[r]
        return carry

    lax.fori_loop(0, width // PAD, mix_tile, 0)

    if not last:
        tail[...] = mix[:, start + width - 2 * PAD : start + width].astype(jnp.bfloat16)
    if first and not last:
        head[...] = mix[:, : 2 * PAD].astype(jnp.bfloat16)
    if first and last:
        mix[:, width:] = mix[:, : 2 * PAD]
        state[:, width:] = state[:, : 2 * PAD]

    lon_tap = [lon_w[k : k + 1] for k in range(TAPS)]
    scale = gain[...]
    made = out.shape[1]

    def rest(at, tile):
        parts = []
        for r in range(rows):
            lon = mix[r, pl.ds(at + PAD - DLON * REACH, tile)] * lon_tap[0]
            for k in range(1, TAPS):
                lon = lon + mix[r, pl.ds(at + PAD + DLON * (k - REACH), tile)] * lon_tap[k]
            parts.append(lon)
        lon = jnp.concatenate(parts, axis=0)
        mean = jnp.mean(lon, axis=-1, keepdims=True)
        centred = lon - mean
        var = jnp.mean(centred * centred, axis=-1, keepdims=True)
        normed = (centred * lax.rsqrt(var + 1e-06) * scale).astype(jnp.bfloat16)
        hidden = jnp.dot(normed, w_in[...], preferred_element_type=jnp.float32)
        hidden = gelu(hidden).astype(jnp.bfloat16)
        delta = jnp.dot(hidden, w_out[...], preferred_element_type=jnp.float32)
        for r in range(rows):
            new = state[r, pl.ds(at + PAD, tile)].astype(jnp.float32) + delta[r * tile : (r + 1) * tile]
            out[r, pl.ds(at, tile)] = new.astype(jnp.bfloat16)

    for at in range(0, made, TILE):
        rest(at, min(TILE, made - at))


def layer_chunk(bands, weights, chunk, prev, first_chunk, first, last):
    own, even_swap, odd_swap = chunk
    rows, width, channels = own.shape
    made = width + (0 if first else PAD) + (0 if last else -PAD) + (PAD if last else 0) - (PAD if first else 0)
    window = made + 2 * PAD
    args = list(weights) + [own, even_swap, odd_swap]
    if not first:
        args += list(prev)
    if last and not first:
        args += list(first_chunk)
    strip = jax.ShapeDtypeStruct((rows, 2 * PAD, channels), jnp.bfloat16)
    outs = [jax.ShapeDtypeStruct((rows, made, channels), jnp.bfloat16)]
    if not last:
        outs.append(strip)
    if first and not last:
        outs.append(strip)
    cells = rows * made
    hidden = weights[3].shape[1]
    return pl.pallas_call(
        functools.partial(chunk_kernel, bands, first, last, width),
        out_shape=outs,
        in_specs=[pl.BlockSpec(memory_space=pltpu.VMEM)] * len(args),
        out_specs=[pl.BlockSpec(memory_space=pltpu.VMEM)] * len(outs),
        scratch_shapes=[
            pltpu.VMEM((rows, window, channels), jnp.float32),
            pltpu.VMEM((rows, window, channels), jnp.bfloat16),
        ],
        compiler_params=pltpu.CompilerParams(vmem_limit_bytes=24 * 2**20),
        cost_estimate=pl.CostEstimate(
            flops=50 * cells * channels * hidden, bytes_accessed=8 * cells * channels, transcendentals=cells * hidden
        ),
    )(*args)


def splits(total):
    first = PAD * ((total // PAD + 4 * LAYERS) // 2)
    return [(0, first), (first, total)]


def swaps(bands, start):
    to = list(range(bands))
    for b in range(start, bands - 1, 2):
        to[b], to[b + 1] = b + 1, b
    return list(enumerate(to))


def member_step(state, weights, bands):
    rows, lons, _ = state.shape
    even_pairs, odd_pairs = swaps(bands, 0), swaps(bands, 1)
    assert rows == REACH
    chunks = [state[:, lo:hi] for lo, hi in splits(lons)]
    for layer in range(LAYERS):
        halos = [(lax.ppermute(own, "band", even_pairs), lax.ppermute(own, "band", odd_pairs)) for own in chunks]
        made, prev, first_chunk = [], None, None
        for c, own in enumerate(chunks):
            first, last = c == 0, c == len(chunks) - 1
            got = layer_chunk(bands, weights[layer], (own,) + halos[c], prev, first_chunk, first, last)
            made.append(got[0])
            if not last:
                prev = (own, got[1])
            if first and not last:
                first_chunk = (own[:, : 2 * PAD], got[2])
        chunks = made
    whole = jnp.concatenate(chunks, axis=1)
    return jnp.roll(whole, LAYERS * PAD, axis=1)


def solution(mesh):
    bands = mesh.shape["band"]

    def shards(fields, lat_taps, lon_taps, gains, w_in, w_out):
        weights = [
            (
                lat_taps[layer].astype(jnp.float32),
                lon_taps[layer].astype(jnp.float32),
                gains[layer : layer + 1],
                w_in[layer],
                w_out[layer],
            )
            for layer in range(LAYERS)
        ]
        return jnp.stack([member_step(fields[m], weights, bands) for m in range(fields.shape[0])])

    return jax.shard_map(
        shards,
        mesh=mesh,
        in_specs=(P(("members", "section"), "band", None, None), P(), P(), P(), P(), P()),
        out_specs=P(("members", "section"), "band", None, None),
        check_vma=False,
    )
```

```python
import functools

import jax
import jax.numpy as jnp
from jax import lax
from jax.experimental import pallas as pl
from jax.experimental.pallas import tpu as pltpu
from jax.sharding import PartitionSpec as P

DLON = 3
LAYERS = 2
TAPS = 9
REACH = TAPS // 2
PAD = 16
TILE = 32


def gelu(x):
    return 0.5 * x * (1.0 + lax.erf(x * 0.7071067811865476))


def chunk_kernel(bands, first, last, width, *refs):
    refs = list(refs)
    lat_w, lon_w, gain, w_in, w_out, own, even_pair, odd_pair = refs[:8]
    refs = refs[8:]
    if not first:
        prev_own, prev_mix = refs[:2]
        refs = refs[2:]
    if last and not first:
        first_own, first_mix = refs[:2]
        refs = refs[2:]
    out = refs.pop(0)
    if not last:
        tail = refs.pop(0)
    if first and not last:
        head = refs.pop(0)
    mix, state = refs
    rows = own.shape[0]
    channels = own.shape[2]
    start = 0 if first else 2 * PAD

    if not first:
        mix[:, : 2 * PAD] = prev_mix[...].astype(jnp.float32)
        state[:, : 2 * PAD] = prev_own[:, prev_own.shape[1] - 2 * PAD :]
    if last and not first:
        mix[:, start + width :] = first_mix[...].astype(jnp.float32)
        state[:, start + width :] = first_own[:, : 2 * PAD]

    band = lax.axis_index("band")
    is_odd = lax.rem(band, 2) == 1
    top, bottom = band == 0, band == bands - 1
    lat_tap = [jnp.broadcast_to(lat_w[k : k + 1], (PAD, channels)) for k in range(TAPS)]

    def mix_tile(t, carry):
        at = pl.multiple_of(t * PAD, PAD)
        to = pl.multiple_of(start + t * PAD, PAD)
        above, below = [], []
        for r in range(REACH):
            here = (r, pl.ds(at, PAD))
            up = jnp.where(is_odd, even_pair[(0,) + here], odd_pair[(0,) + here])
            down = jnp.where(is_odd, odd_pair[(1,) + here], even_pair[(1,) + here])
            above.append(jnp.where(top, jnp.zeros_like(up), up))
            below.append(jnp.where(bottom, jnp.zeros_like(down), down))
        mine = [own[r, pl.ds(at, PAD)] for r in range(rows)]
        strip = [s.astype(jnp.float32) for s in above + mine + below]
        for r in range(rows):
            total = strip[r] * lat_tap[0]
            for k in range(1, TAPS):
                total = total + strip[r + k] * lat_tap[k]
            mix[r, pl.ds(to, PAD)] = total.astype(jnp.bfloat16).astype(jnp.float32)
            state[r, pl.ds(to, PAD)] = mine[r]
        return carry

    lax.fori_loop(0, width // PAD, mix_tile, 0)

    if not last:
        tail[...] = mix[:, start + width - 2 * PAD : start + width].astype(jnp.bfloat16)
    if first and not last:
        head[...] = mix[:, : 2 * PAD].astype(jnp.bfloat16)
    if first and last:
        mix[:, width:] = mix[:, : 2 * PAD]
        state[:, width:] = state[:, : 2 * PAD]

    lon_tap = [lon_w[k : k + 1] for k in range(TAPS)]
    scale = gain[...]
    made = out.shape[1]

    def rest(at, tile):
        parts = []
        for r in range(rows):
            lon = mix[r, pl.ds(at + PAD - DLON * REACH, tile)] * lon_tap[0]
            for k in range(1, TAPS):
                lon = lon + mix[r, pl.ds(at + PAD + DLON * (k - REACH), tile)] * lon_tap[k]
            parts.append(lon)
        lon = jnp.concatenate(parts, axis=0)
        mean = jnp.mean(lon, axis=-1, keepdims=True)
        centred = lon - mean
        var = jnp.mean(centred * centred, axis=-1, keepdims=True)
        normed = (centred * lax.rsqrt(var + 1e-06) * scale).astype(jnp.bfloat16)
        hidden = jnp.dot(normed, w_in[...], preferred_element_type=jnp.float32)
        hidden = gelu(hidden).astype(jnp.bfloat16)
        delta = jnp.dot(hidden, w_out[...], preferred_element_type=jnp.float32)
        for r in range(rows):
            new = state[r, pl.ds(at + PAD, tile)].astype(jnp.float32) + delta[r * tile : (r + 1) * tile]
            out[r, pl.ds(at, tile)] = new.astype(jnp.bfloat16)

    for at in range(0, made, TILE):
        rest(at, min(TILE, made - at))


def layer_chunk(bands, weights, chunk, prev, first_chunk, first, last):
    own, even_pair, odd_pair = chunk
    rows, width, channels = own.shape
    made = width + (0 if first else PAD) + (0 if last else -PAD) + (PAD if last else 0) - (PAD if first else 0)
    window = made + 2 * PAD
    args = list(weights) + [own, even_pair, odd_pair]
    if not first:
        args += list(prev)
    if last and not first:
        args += list(first_chunk)
    strip = jax.ShapeDtypeStruct((rows, 2 * PAD, channels), jnp.bfloat16)
    outs = [jax.ShapeDtypeStruct((rows, made, channels), jnp.bfloat16)]
    if not last:
        outs.append(strip)
    if first and not last:
        outs.append(strip)
    cells = rows * made
    hidden = weights[3].shape[1]
    return pl.pallas_call(
        functools.partial(chunk_kernel, bands, first, last, width),
        out_shape=outs,
        in_specs=[pl.BlockSpec(memory_space=pltpu.VMEM)] * len(args),
        out_specs=[pl.BlockSpec(memory_space=pltpu.VMEM)] * len(outs),
        scratch_shapes=[
            pltpu.VMEM((rows, window, channels), jnp.float32),
            pltpu.VMEM((rows, window, channels), jnp.bfloat16),
        ],
        compiler_params=pltpu.CompilerParams(vmem_limit_bytes=24 * 2**20),
        cost_estimate=pl.CostEstimate(
            flops=50 * cells * channels * hidden, bytes_accessed=8 * cells * channels, transcendentals=cells * hidden
        ),
    )(*args)


def splits(total):
    first = PAD * ((total // PAD + 4 * LAYERS) // 2)
    return [(0, first), (first, total)]


def pairs(bands, cores, start):
    groups, alone = [], list(range(bands))
    for b in range(start, bands - 1, 2):
        groups += [[b * cores + m, (b + 1) * cores + m] for m in range(cores)]
        alone.remove(b)
        alone.remove(b + 1)
    return groups + [[b * cores, b * cores + 1] for b in alone]


def member_step(state, weights, bands, cores):
    rows, lons, _ = state.shape
    both = [pairs(bands, cores, start) for start in (0, 1)]
    assert rows == REACH
    chunks = [state[:, lo:hi] for lo, hi in splits(lons)]
    for layer in range(LAYERS):
        halos = [
            [lax.all_gather(own, ("band", "members"), axis_index_groups=groups) for groups in both] for own in chunks
        ]
        made, prev, first_chunk = [], None, None
        for c, own in enumerate(chunks):
            first, last = c == 0, c == len(chunks) - 1
            got = layer_chunk(bands, weights[layer], [own] + halos[c], prev, first_chunk, first, last)
            made.append(got[0])
            if not last:
                prev = (own, got[1])
            if first and not last:
                first_chunk = (own[:, : 2 * PAD], got[2])
        chunks = made
    whole = jnp.concatenate(chunks, axis=1)
    return jnp.roll(whole, LAYERS * PAD, axis=1)


def solution(mesh):
    bands, cores = mesh.shape["band"], mesh.shape["members"]
    assert cores == 2

    def shards(fields, lat_taps, lon_taps, gains, w_in, w_out):
        weights = [
            (
                lat_taps[layer].astype(jnp.float32),
                lon_taps[layer].astype(jnp.float32),
                gains[layer : layer + 1],
                w_in[layer],
                w_out[layer],
            )
            for layer in range(LAYERS)
        ]
        return jnp.stack([member_step(fields[m], weights, bands, cores) for m in range(fields.shape[0])])

    return jax.shard_map(
        shards,
        mesh=mesh,
        in_specs=(P(("members", "section"), "band", None, None), P(), P(), P(), P(), P()),
        out_specs=P(("members", "section"), "band", None, None),
        check_vma=False,
    )
```

```python
import functools

import jax
import jax.numpy as jnp
from jax import lax
from jax.experimental import pallas as pl
from jax.experimental.pallas import tpu as pltpu
from jax.sharding import PartitionSpec as P

DLON = 3
LAYERS = 2
TAPS = 9
REACH = TAPS // 2
PAD = 16
TILE = 32
ERFC_POWER = (
    -1.000037622280944,
    -1.1507878529643598,
    -0.459992437236149,
    -0.051827384082804726,
    0.007084557514732341,
    -0.00047330932043343645,
)


def gelu(x):
    size = jnp.abs(x)
    power = ERFC_POWER[-1] * size + ERFC_POWER[-2]
    for c in ERFC_POWER[-3::-1]:
        power = power * size + c
    return jnp.maximum(x, 0.0) - size * jnp.exp2(power)


def own_kernel(ranges, lat_w, state, *outs):
    rows, channels = state.shape[0], state.shape[2]
    lat_tap = [jnp.broadcast_to(lat_w[k : k + 1], (PAD, channels)) for k in range(TAPS)]
    for (lo, hi), sums in zip(ranges, outs[: len(ranges)]):

        def tile(t, carry):
            at = pl.multiple_of(t * PAD, PAD)
            here = pl.multiple_of(lo + t * PAD, PAD)
            own = [state[r, pl.ds(here, PAD)].astype(jnp.float32) for r in range(rows)]
            for r in range(rows):
                total = own[0] * lat_tap[REACH - r]
                for k in range(1, rows):
                    total = total + own[k] * lat_tap[REACH - r + k]
                sums[r, pl.ds(at, PAD)] = total
            return carry

        lax.fori_loop(0, (hi - lo) // PAD, tile, 0)
    for (lo, hi), copy in zip(ranges[1:], outs[len(ranges) :]):
        copy[...] = state[:, lo:hi]


def own_share(lat_w, state, ranges):
    rows, _, channels = state.shape
    shapes = [jax.ShapeDtypeStruct((rows, hi - lo, channels), jnp.float32) for lo, hi in ranges]
    shapes += [jax.ShapeDtypeStruct((rows, hi - lo, channels), jnp.bfloat16) for lo, hi in ranges[1:]]
    cells = rows * state.shape[1]
    got = pl.pallas_call(
        functools.partial(own_kernel, ranges),
        out_shape=shapes,
        in_specs=[pl.BlockSpec(memory_space=pltpu.VMEM)] * 2,
        out_specs=[pl.BlockSpec(memory_space=pltpu.VMEM)] * len(shapes),
        compiler_params=pltpu.CompilerParams(vmem_limit_bytes=16 * 2**20),
        cost_estimate=pl.CostEstimate(
            flops=3200 * cells * channels, bytes_accessed=8 * cells * channels, transcendentals=0
        ),
    )(lat_w, state)
    return list(got[: len(ranges)]), list(got[len(ranges) :])


def chunk_kernel(bands, first, last, width, place, *refs):
    refs = list(refs)
    lat_w, lon_w, gain, w_in, w_out, own, sums, even_swap, odd_swap = refs[:9]
    refs = refs[9:]
    if not first:
        prev_own, prev_mix = refs[:2]
        refs = refs[2:]
    if last and not first:
        first_own, first_mix = refs[:2]
        refs = refs[2:]
    if place is not None and not first:
        refs.pop(0)
    out = refs.pop(0)
    if not last:
        tail = refs.pop(0)
    if first and not last:
        head = refs.pop(0)
    mix, state = refs[:2]
    whole = out
    if place is not None:
        out, sems = refs[2:]
    rows = own.shape[0]
    channels = own.shape[2]
    start = 0 if first else 2 * PAD

    if not first:
        mix[:, : 2 * PAD] = prev_mix[...].astype(jnp.float32)
        state[:, : 2 * PAD] = prev_own[:, prev_own.shape[1] - 2 * PAD :]
    if last and not first:
        mix[:, start + width :] = first_mix[...].astype(jnp.float32)
        state[:, start + width :] = first_own[:, : 2 * PAD]

    band = lax.axis_index("band")
    is_odd = lax.rem(band, 2) == 1
    lat_tap = [jnp.broadcast_to(lat_w[k : k + 1], (PAD, channels)) for k in range(TAPS)]

    def mix_tile(t, carry):
        at = pl.multiple_of(t * PAD, PAD)
        to = pl.multiple_of(start + t * PAD, PAD)
        evens = [even_swap[r, pl.ds(at, PAD)] for r in range(REACH)]
        odds = [odd_swap[r, pl.ds(at, PAD)] for r in range(REACH)]
        above = [jnp.where(is_odd, e, o) for e, o in zip(evens, odds)]
        below = [jnp.where(is_odd, o, e) for e, o in zip(evens, odds)]
        above = [s.astype(jnp.float32) for s in above]
        below = [s.astype(jnp.float32) for s in below]
        for r in range(rows):
            total = sums[r, pl.ds(at, PAD)]
            for k in range(REACH - r):
                total = total + above[r + k] * lat_tap[k]
            for k in range(TAPS - 1 - r, TAPS):
                total = total + below[r + k - TAPS + 1] * lat_tap[k]
            mix[r, pl.ds(to, PAD)] = total.astype(jnp.bfloat16).astype(jnp.float32)
            state[r, pl.ds(to, PAD)] = own[r, pl.ds(at, PAD)]
        return carry

    lax.fori_loop(0, width // PAD, mix_tile, 0)

    if not last:
        tail[...] = mix[:, start + width - 2 * PAD : start + width].astype(jnp.bfloat16)
    if first and not last:
        head[...] = mix[:, : 2 * PAD].astype(jnp.bfloat16)
    if first and last:
        mix[:, width:] = mix[:, : 2 * PAD]
        state[:, width:] = state[:, : 2 * PAD]

    lon_tap = [lon_w[k : k + 1] for k in range(TAPS)]
    scale = gain[...]
    made, total = out.shape[1], whole.shape[1]

    def rest(at, tile):
        parts = []
        for r in range(rows):
            lon = mix[r, pl.ds(at + PAD - DLON * REACH, tile)] * lon_tap[0]
            for k in range(1, TAPS):
                lon = lon + mix[r, pl.ds(at + PAD + DLON * (k - REACH), tile)] * lon_tap[k]
            parts.append(lon)
        lon = jnp.concatenate(parts, axis=0)
        mean = jnp.mean(lon, axis=-1, keepdims=True)
        centred = lon - mean
        var = jnp.mean(centred * centred, axis=-1, keepdims=True)
        normed = (centred * lax.rsqrt(var + 1e-06) * scale).astype(jnp.bfloat16)
        hidden = jnp.dot(normed, w_in[...], preferred_element_type=jnp.float32)
        hidden = gelu(hidden).astype(jnp.bfloat16)
        delta = jnp.dot(hidden, w_out[...], preferred_element_type=jnp.float32)
        for r in range(rows):
            new = state[r, pl.ds(at + PAD, tile)].astype(jnp.float32) + delta[r * tile : (r + 1) * tile]
            out[r, pl.ds(at, tile)] = new.astype(jnp.bfloat16)

    copies = []
    for at, tile in tiles(made):
        rest(at, tile)
        if place is not None:
            to = (place + at) % total
            copies.append(
                pltpu.make_async_copy(out.at[:, at : at + tile], whole.at[:, to : to + tile], sems.at[len(copies)])
            )
            copies[-1].start()
    for copy in copies:
        copy.wait()


def tiles(made):
    return [(at, min(TILE, made - at)) for at in range(0, made, TILE)]


def layer_chunk(bands, weights, chunk, prev, first_chunk, first, last, place=None, whole=None):
    own = chunk[0]
    rows, width, channels = own.shape
    made = width + (0 if first else PAD) + (0 if last else -PAD) + (PAD if last else 0) - (PAD if first else 0)
    window = made + 2 * PAD
    args = list(weights) + list(chunk)
    if not first:
        args += list(prev)
    if last and not first:
        args += list(first_chunk)
    specs = [pl.BlockSpec(memory_space=pltpu.VMEM)] * len(args)
    strip = jax.ShapeDtypeStruct((rows, 2 * PAD, channels), jnp.bfloat16)
    outs = [jax.ShapeDtypeStruct((rows, made, channels), jnp.bfloat16)]
    out_specs = [pl.BlockSpec(memory_space=pltpu.VMEM)]
    scratch = [
        pltpu.VMEM((rows, window, channels), jnp.float32),
        pltpu.VMEM((rows, window, channels), jnp.bfloat16),
    ]
    aliases = {}
    if place is not None:
        scratch += [pltpu.VMEM(outs[0].shape, jnp.bfloat16), pltpu.SemaphoreType.DMA((len(tiles(made)),))]
        outs = [jax.ShapeDtypeStruct((rows, whole if first else whole.shape[1], channels), jnp.bfloat16)]
        out_specs = [pl.BlockSpec(memory_space=pltpu.HBM)]
        if not first:
            aliases = {len(args): 0}
            args.append(whole)
            specs += out_specs
    if not last:
        outs.append(strip)
    if first and not last:
        outs.append(strip)
    out_specs += [pl.BlockSpec(memory_space=pltpu.VMEM)] * (len(outs) - 1)
    cells = rows * made
    hidden = weights[3].shape[1]
    return pl.pallas_call(
        functools.partial(chunk_kernel, bands, first, last, width, place),
        out_shape=outs,
        in_specs=specs,
        out_specs=out_specs,
        scratch_shapes=scratch,
        input_output_aliases=aliases,
        compiler_params=pltpu.CompilerParams(vmem_limit_bytes=24 * 2**20),
        cost_estimate=pl.CostEstimate(
            flops=50 * cells * channels * hidden, bytes_accessed=8 * cells * channels, transcendentals=cells * hidden
        ),
    )(*args)


def splits(total):
    first = PAD * ((total // PAD + 4 * LAYERS) // 2)
    return [(0, first), (first, total)]


def swaps(bands, start):
    return [pair for b in range(start, bands - 1, 2) for pair in ((b, b + 1), (b + 1, b))]


def member_step(state, weights, bands):
    rows, lons, _ = state.shape
    assert rows == REACH
    even_pairs, odd_pairs = swaps(bands, 0), swaps(bands, 1)
    ranges = splits(lons)
    sums, later = own_share(weights[0][0], state, ranges)
    chunks = [state[:, : ranges[0][1]]] + later
    whole, place = lons, LAYERS * PAD
    for layer in range(LAYERS):
        halos = [(lax.ppermute(own, "band", even_pairs), lax.ppermute(own, "band", odd_pairs)) for own in chunks]
        if layer > 0:
            sums = [own_share(weights[layer][0], own, [(0, own.shape[1])])[0][0] for own in chunks]
        final = layer == LAYERS - 1
        made, prev, first_chunk = [], None, None
        for c, own in enumerate(chunks):
            first, last = c == 0, c == len(chunks) - 1
            where = (place, whole) if final else ()
            got = layer_chunk(bands, weights[layer], (own, sums[c]) + halos[c], prev, first_chunk, first, last, *where)
            made.append(got[0])
            if final:
                whole = got[0]
                place += own.shape[1] - (2 * PAD if first else 0)
            if not last:
                prev = (own, got[1])
            if first and not last:
                first_chunk = (own[:, : 2 * PAD], got[2])
        chunks = made
    return whole


def solution(mesh):
    bands = mesh.shape["band"]

    def shards(fields, lat_taps, lon_taps, gains, w_in, w_out):
        weights = [
            (
                lat_taps[layer].astype(jnp.float32),
                lon_taps[layer].astype(jnp.float32),
                gains[layer : layer + 1],
                w_in[layer],
                w_out[layer],
            )
            for layer in range(LAYERS)
        ]
        return jnp.concatenate([member_step(fields[m], weights, bands)[None] for m in range(fields.shape[0])])

    return jax.shard_map(
        shards,
        mesh=mesh,
        in_specs=(P(("members", "section"), "band", None, None), P(), P(), P(), P(), P()),
        out_specs=P(("members", "section"), "band", None, None),
        check_vma=False,
    )
```

```python
import functools

import jax
import jax.numpy as jnp
from jax import lax
from jax.experimental import pallas as pl
from jax.experimental.pallas import tpu as pltpu
from jax.sharding import PartitionSpec as P

DLON = 3
LAYERS = 2
TAPS = 9
REACH = TAPS // 2
PAD = 16
TILE = 48
NORM_TILE = 32
ERFC_POWER = (
    -1.000037622280944,
    -1.1507878529643598,
    -0.459992437236149,
    -0.051827384082804726,
    0.007084557514732341,
    -0.00047330932043343645,
)


def gelu(x):
    size = jnp.abs(x)
    power = ERFC_POWER[-1] * size + ERFC_POWER[-2]
    for c in ERFC_POWER[-3::-1]:
        power = power * size + c
    return jnp.maximum(x, 0.0) - size * jnp.exp2(power)


def own_kernel(ranges, lat_w, state, *outs):
    rows, channels = state.shape[0], state.shape[2]
    lat_tap = [jnp.broadcast_to(lat_w[k : k + 1], (PAD, channels)) for k in range(TAPS)]
    for (lo, hi), sums in zip(ranges, outs[: len(ranges)]):

        def tile(t, carry):
            at = pl.multiple_of(t * PAD, PAD)
            here = pl.multiple_of(lo + t * PAD, PAD)
            own = [state[r, pl.ds(here, PAD)].astype(jnp.float32) for r in range(rows)]
            for r in range(rows):
                total = own[0] * lat_tap[REACH - r]
                for k in range(1, rows):
                    total = total + own[k] * lat_tap[REACH - r + k]
                sums[r, pl.ds(at, PAD)] = total
            return carry

        lax.fori_loop(0, (hi - lo) // PAD, tile, 0)
    for (lo, hi), copy in zip(ranges[1:], outs[len(ranges) :]):
        copy[...] = state[:, lo:hi]


def own_share(lat_w, state, ranges):
    rows, _, channels = state.shape
    shapes = [jax.ShapeDtypeStruct((rows, hi - lo, channels), jnp.float32) for lo, hi in ranges]
    shapes += [jax.ShapeDtypeStruct((rows, hi - lo, channels), jnp.bfloat16) for lo, hi in ranges[1:]]
    cells = rows * state.shape[1]
    got = pl.pallas_call(
        functools.partial(own_kernel, ranges),
        out_shape=shapes,
        in_specs=[pl.BlockSpec(memory_space=pltpu.VMEM)] * 2,
        out_specs=[pl.BlockSpec(memory_space=pltpu.VMEM)] * len(shapes),
        compiler_params=pltpu.CompilerParams(vmem_limit_bytes=16 * 2**20),
        cost_estimate=pl.CostEstimate(
            flops=3200 * cells * channels, bytes_accessed=8 * cells * channels, transcendentals=0
        ),
    )(lat_w, state)
    return list(got[: len(ranges)]), list(got[len(ranges) :])


def chunk_kernel(bands, first, last, width, place, *refs):
    refs = list(refs)
    lat_w, lon_w, gain, w_in, w_out, own, sums, even_swap, odd_swap = refs[:9]
    refs = refs[9:]
    if not first:
        prev_own, prev_mix = refs[:2]
        refs = refs[2:]
    if last and not first:
        first_own, first_mix = refs[:2]
        refs = refs[2:]
    if place is not None and not first:
        refs.pop(0)
    out = refs.pop(0)
    if not last:
        tail = refs.pop(0)
    if first and not last:
        head = refs.pop(0)
    mix, state, normed = refs[:3]
    whole = out
    if place is not None:
        out, sems = refs[3:]
    rows = own.shape[0]
    channels = own.shape[2]
    start = 0 if first else 2 * PAD

    if not first:
        mix[:, : 2 * PAD] = prev_mix[...].astype(jnp.float32)
        state[:, : 2 * PAD] = prev_own[:, prev_own.shape[1] - 2 * PAD :]
    if last and not first:
        mix[:, start + width :] = first_mix[...].astype(jnp.float32)
        state[:, start + width :] = first_own[:, : 2 * PAD]

    band = lax.axis_index("band")
    is_odd = lax.rem(band, 2) == 1
    lat_tap = [jnp.broadcast_to(lat_w[k : k + 1], (PAD, channels)) for k in range(TAPS)]

    def mix_tile(t, carry):
        at = pl.multiple_of(t * PAD, PAD)
        to = pl.multiple_of(start + t * PAD, PAD)
        evens = [even_swap[r, pl.ds(at, PAD)] for r in range(REACH)]
        odds = [odd_swap[r, pl.ds(at, PAD)] for r in range(REACH)]
        above = [jnp.where(is_odd, e, o) for e, o in zip(evens, odds)]
        below = [jnp.where(is_odd, o, e) for e, o in zip(evens, odds)]
        above = [s.astype(jnp.float32) for s in above]
        below = [s.astype(jnp.float32) for s in below]
        for r in range(rows):
            total = sums[r, pl.ds(at, PAD)]
            for k in range(REACH - r):
                total = total + above[r + k] * lat_tap[k]
            for k in range(TAPS - 1 - r, TAPS):
                total = total + below[r + k - TAPS + 1] * lat_tap[k]
            mix[r, pl.ds(to, PAD)] = total.astype(jnp.bfloat16).astype(jnp.float32)
            state[r, pl.ds(to, PAD)] = own[r, pl.ds(at, PAD)]
        return carry

    lax.fori_loop(0, width // PAD, mix_tile, 0)

    if not last:
        tail[...] = mix[:, start + width - 2 * PAD : start + width].astype(jnp.bfloat16)
    if first and not last:
        head[...] = mix[:, : 2 * PAD].astype(jnp.bfloat16)
    if first and last:
        mix[:, width:] = mix[:, : 2 * PAD]
        state[:, width:] = state[:, : 2 * PAD]

    lon_tap = [lon_w[k : k + 1] for k in range(TAPS)]
    scale = gain[...]
    made, total = out.shape[1], whole.shape[1]

    def norm_tile(t, carry):
        at = t * NORM_TILE
        parts = []
        for r in range(rows):
            lon = mix[r, pl.ds(at + PAD - DLON * REACH, NORM_TILE)] * lon_tap[0]
            for k in range(1, TAPS):
                lon = lon + mix[r, pl.ds(at + PAD + DLON * (k - REACH), NORM_TILE)] * lon_tap[k]
            parts.append(lon)
        lon = jnp.concatenate(parts, axis=0)
        mean = jnp.mean(lon, axis=-1, keepdims=True)
        centred = lon - mean
        var = jnp.mean(centred * centred, axis=-1, keepdims=True)
        unit = (centred * lax.rsqrt(var + 1e-06) * scale).astype(jnp.bfloat16)
        for r in range(rows):
            normed[r, pl.ds(pl.multiple_of(at, NORM_TILE), NORM_TILE)] = unit[r * NORM_TILE : (r + 1) * NORM_TILE]
        return carry

    lax.fori_loop(0, made // NORM_TILE, norm_tile, 0)

    def rest(at, tile):
        flat = jnp.concatenate([normed[r, at : at + tile] for r in range(rows)], axis=0)
        hidden = jnp.dot(flat, w_in[...], preferred_element_type=jnp.float32)
        hidden = gelu(hidden).astype(jnp.bfloat16)
        delta = jnp.dot(hidden, w_out[...], preferred_element_type=jnp.float32)
        for r in range(rows):
            new = state[r, at + PAD : at + PAD + tile].astype(jnp.float32) + delta[r * tile : (r + 1) * tile]
            out[r, at : at + tile] = new.astype(jnp.bfloat16)

    copies = []
    for at, tile in tiles(made, total, place):
        rest(at, tile)
        if place is not None:
            to = (place + at) % total
            copies.append(
                pltpu.make_async_copy(out.at[:, at : at + tile], whole.at[:, to : to + tile], sems.at[len(copies)])
            )
            copies[-1].start()
    for copy in copies:
        copy.wait()


def tiles(made, total, place):
    edges = set(range(0, made, TILE)) | {made}
    if place is not None and place + made > total:
        edges = set(range(0, total - place, TILE)) | set(range(total - place, made, TILE)) | {made}
    edges = sorted(edges)
    return [(lo, hi - lo) for lo, hi in zip(edges[:-1], edges[1:])]


def layer_chunk(bands, weights, chunk, prev, first_chunk, first, last, place=None, whole=None):
    own = chunk[0]
    rows, width, channels = own.shape
    made = width + (0 if first else PAD) + (0 if last else -PAD) + (PAD if last else 0) - (PAD if first else 0)
    window = made + 2 * PAD
    args = list(weights) + list(chunk)
    if not first:
        args += list(prev)
    if last and not first:
        args += list(first_chunk)
    specs = [pl.BlockSpec(memory_space=pltpu.VMEM)] * len(args)
    strip = jax.ShapeDtypeStruct((rows, 2 * PAD, channels), jnp.bfloat16)
    outs = [jax.ShapeDtypeStruct((rows, made, channels), jnp.bfloat16)]
    out_specs = [pl.BlockSpec(memory_space=pltpu.VMEM)]
    scratch = [
        pltpu.VMEM((rows, window, channels), jnp.float32),
        pltpu.VMEM((rows, window, channels), jnp.bfloat16),
        pltpu.VMEM((rows, made, channels), jnp.bfloat16),
    ]
    aliases = {}
    if place is not None:
        lons = whole if first else whole.shape[1]
        scratch += [pltpu.VMEM(outs[0].shape, jnp.bfloat16), pltpu.SemaphoreType.DMA((len(tiles(made, lons, place)),))]
        outs = [jax.ShapeDtypeStruct((rows, lons, channels), jnp.bfloat16)]
        out_specs = [pl.BlockSpec(memory_space=pltpu.HBM)]
        if not first:
            aliases = {len(args): 0}
            args.append(whole)
            specs += out_specs
    if not last:
        outs.append(strip)
    if first and not last:
        outs.append(strip)
    out_specs += [pl.BlockSpec(memory_space=pltpu.VMEM)] * (len(outs) - 1)
    cells = rows * made
    hidden = weights[3].shape[1]
    return pl.pallas_call(
        functools.partial(chunk_kernel, bands, first, last, width, place),
        out_shape=outs,
        in_specs=specs,
        out_specs=out_specs,
        scratch_shapes=scratch,
        input_output_aliases=aliases,
        compiler_params=pltpu.CompilerParams(vmem_limit_bytes=24 * 2**20),
        cost_estimate=pl.CostEstimate(
            flops=50 * cells * channels * hidden, bytes_accessed=8 * cells * channels, transcendentals=cells * hidden
        ),
    )(*args)


def splits(total):
    first = 2 * PAD * ((total // PAD + 2 * LAYERS) // 4)
    return [(0, first), (first, total)]


def swaps(bands, start):
    return [pair for b in range(start, bands - 1, 2) for pair in ((b, b + 1), (b + 1, b))]


def member_step(state, weights, bands):
    rows, lons, _ = state.shape
    assert rows == REACH
    even_pairs, odd_pairs = swaps(bands, 0), swaps(bands, 1)
    ranges = splits(lons)
    sums, later = own_share(weights[0][0], state, ranges)
    chunks = [state[:, : ranges[0][1]]] + later
    whole, place = lons, LAYERS * PAD
    for layer in range(LAYERS):
        halos = [(lax.ppermute(own, "band", even_pairs), lax.ppermute(own, "band", odd_pairs)) for own in chunks]
        if layer > 0:
            sums = [own_share(weights[layer][0], own, [(0, own.shape[1])])[0][0] for own in chunks]
        final = layer == LAYERS - 1
        made, prev, first_chunk = [], None, None
        for c, own in enumerate(chunks):
            first, last = c == 0, c == len(chunks) - 1
            where = (place, whole) if final else ()
            got = layer_chunk(bands, weights[layer], (own, sums[c]) + halos[c], prev, first_chunk, first, last, *where)
            made.append(got[0])
            if final:
                whole = got[0]
                place += own.shape[1] - (2 * PAD if first else 0)
            if not last:
                prev = (own, got[1])
            if first and not last:
                first_chunk = (own[:, : 2 * PAD], got[2])
        chunks = made
    return whole


def solution(mesh):
    bands = mesh.shape["band"]

    def shards(fields, lat_taps, lon_taps, gains, w_in, w_out):
        weights = [
            (
                lat_taps[layer].astype(jnp.float32),
                lon_taps[layer].astype(jnp.float32),
                gains[layer : layer + 1],
                w_in[layer],
                w_out[layer],
            )
            for layer in range(LAYERS)
        ]
        return jnp.concatenate([member_step(fields[m], weights, bands)[None] for m in range(fields.shape[0])])

    return jax.shard_map(
        shards,
        mesh=mesh,
        in_specs=(P(("members", "section"), "band", None, None), P(), P(), P(), P(), P()),
        out_specs=P(("members", "section"), "band", None, None),
        check_vma=False,
    )
```

```python
import functools

import jax
import jax.numpy as jnp
from jax import lax
from jax.experimental import pallas as pl
from jax.experimental.pallas import tpu as pltpu
from jax.sharding import PartitionSpec as P

DLON = 3
LAYERS = 2
TAPS = 9
REACH = TAPS // 2
PAD = 16
TILE = 64
ERFC_POWER = (
    -1.000037622280944,
    -1.1507878529643598,
    -0.459992437236149,
    -0.051827384082804726,
    0.007084557514732341,
    -0.00047330932043343645,
)


def gelu(x):
    size = jnp.abs(x)
    power = ERFC_POWER[-1] * size + ERFC_POWER[-2]
    for c in ERFC_POWER[-3::-1]:
        power = power * size + c
    return jnp.maximum(x, 0.0) - size * jnp.exp2(power)


def own_kernel(lo, lat_w, state, *refs):
    sums = refs[-2]
    refs[-1][...] = state[:, lo : lo + sums.shape[1]]
    rows, channels = state.shape[0], state.shape[2]
    lat_tap = [jnp.broadcast_to(lat_w[k : k + 1], (PAD, channels)) for k in range(TAPS)]

    def tile(t, carry):
        at = pl.multiple_of(t * PAD, PAD)
        here = pl.multiple_of(lo + t * PAD, PAD)
        own = [state[r, pl.ds(here, PAD)].astype(jnp.float32) for r in range(rows)]
        for r in range(rows):
            total = own[0] * lat_tap[REACH - r]
            for k in range(1, rows):
                total = total + own[k] * lat_tap[REACH - r + k]
            sums[r, pl.ds(at, PAD)] = total
        return carry

    lax.fori_loop(0, sums.shape[1] // PAD, tile, 0)


def own_share(lat_w, state, lo, hi, after):
    rows, _, channels = state.shape
    shape = (rows, hi - lo, channels)
    cells = rows * (hi - lo)
    return pl.pallas_call(
        functools.partial(own_kernel, lo),
        out_shape=[jax.ShapeDtypeStruct(shape, jnp.float32), jax.ShapeDtypeStruct(shape, jnp.bfloat16)],
        in_specs=[pl.BlockSpec(memory_space=pltpu.VMEM)] * 2 + [pl.BlockSpec(memory_space=pl.ANY)] * len(after),
        out_specs=[pl.BlockSpec(memory_space=pltpu.VMEM)] * 2,
        compiler_params=pltpu.CompilerParams(vmem_limit_bytes=16 * 2**20),
        cost_estimate=pl.CostEstimate(
            flops=3200 * cells * channels, bytes_accessed=8 * cells * channels, transcendentals=0
        ),
    )(lat_w, state, *after)


def first_kernel(state, out, sem):
    copy = pltpu.make_async_copy(state.at[:, : out.shape[1]], out, sem)
    copy.start()
    copy.wait()


def first_columns(state, width):
    return pl.pallas_call(
        first_kernel,
        out_shape=jax.ShapeDtypeStruct((state.shape[0], width, state.shape[2]), state.dtype),
        in_specs=[pl.BlockSpec(memory_space=pltpu.HBM)],
        out_specs=pl.BlockSpec(memory_space=pltpu.VMEM),
        scratch_shapes=[pltpu.SemaphoreType.DMA],
    )(state)


def chunk_kernel(bands, first, last, width, place, *refs):
    refs = list(refs)
    lat_w, lon_w, gain, w_in, w_out, own, sums, even_swap, odd_swap = refs[:9]
    refs = refs[9:]
    if not first:
        prev_own, prev_mix = refs[:2]
        refs = refs[2:]
    if last and not first:
        first_own, first_mix = refs[:2]
        refs = refs[2:]
    if place is not None and not first:
        refs.pop(0)
    out = refs.pop(0)
    if not last:
        tail = refs.pop(0)
    if first and not last:
        head = refs.pop(0)
    mix, state = refs[:2]
    whole = out
    if place is not None:
        out, sems = refs[2:]
    rows = own.shape[0]
    channels = own.shape[2]
    start = 0 if first else 2 * PAD

    if not first:
        mix[:, : 2 * PAD] = prev_mix[...].astype(jnp.float32)
        state[:, : 2 * PAD] = prev_own[:, prev_own.shape[1] - 2 * PAD :]
    if last and not first:
        mix[:, start + width :] = first_mix[...].astype(jnp.float32)
        state[:, start + width :] = first_own[:, : 2 * PAD]

    band = lax.axis_index("band")
    is_odd = lax.rem(band, 2) == 1
    lat_tap = [jnp.broadcast_to(lat_w[k : k + 1], (PAD, channels)) for k in range(TAPS)]

    def mix_tile(t, carry):
        at = pl.multiple_of(t * PAD, PAD)
        to = pl.multiple_of(start + t * PAD, PAD)
        evens = [even_swap[r, pl.ds(at, PAD)] for r in range(REACH)]
        odds = [odd_swap[r, pl.ds(at, PAD)] for r in range(REACH)]
        above = [jnp.where(is_odd, e, o) for e, o in zip(evens, odds)]
        below = [jnp.where(is_odd, o, e) for e, o in zip(evens, odds)]
        above = [s.astype(jnp.float32) for s in above]
        below = [s.astype(jnp.float32) for s in below]
        for r in range(rows):
            total = sums[r, pl.ds(at, PAD)]
            for k in range(REACH - r):
                total = total + above[r + k] * lat_tap[k]
            for k in range(TAPS - 1 - r, TAPS):
                total = total + below[r + k - TAPS + 1] * lat_tap[k]
            mix[r, pl.ds(to, PAD)] = total.astype(jnp.bfloat16).astype(jnp.float32)
            state[r, pl.ds(to, PAD)] = own[r, pl.ds(at, PAD)]
        return carry

    lax.fori_loop(0, width // PAD, mix_tile, 0)

    if not last:
        tail[...] = mix[:, start + width - 2 * PAD : start + width].astype(jnp.bfloat16)
    if first and not last:
        head[...] = mix[:, : 2 * PAD].astype(jnp.bfloat16)
    if first and last:
        mix[:, width:] = mix[:, : 2 * PAD]
        state[:, width:] = state[:, : 2 * PAD]

    lon_tap = [lon_w[k : k + 1] for k in range(TAPS)]
    scale = gain[...]
    made, total = out.shape[1], whole.shape[1]

    def rest(at, tile):
        parts = []
        for r in range(rows):
            lon = mix[r, pl.ds(at + PAD - DLON * REACH, tile)] * lon_tap[0]
            for k in range(1, TAPS):
                lon = lon + mix[r, pl.ds(at + PAD + DLON * (k - REACH), tile)] * lon_tap[k]
            parts.append(lon)
        lon = jnp.concatenate(parts, axis=0)
        mean = jnp.mean(lon, axis=-1, keepdims=True)
        centred = lon - mean
        var = jnp.mean(centred * centred, axis=-1, keepdims=True)
        normed = (centred * lax.rsqrt(var + 1e-06) * scale).astype(jnp.bfloat16)
        hidden = jnp.dot(normed, w_in[...], preferred_element_type=jnp.float32)
        hidden = gelu(hidden).astype(jnp.bfloat16)
        delta = jnp.dot(hidden, w_out[...], preferred_element_type=jnp.float32)
        for r in range(rows):
            new = state[r, pl.ds(at + PAD, tile)].astype(jnp.float32) + delta[r * tile : (r + 1) * tile]
            out[r, pl.ds(at, tile)] = new.astype(jnp.bfloat16)

    copies = []
    for at, tile in tiles(made, total, place):
        rest(at, tile)
        if place is not None:
            to = (place + at) % total
            copies.append(
                pltpu.make_async_copy(out.at[:, at : at + tile], whole.at[:, to : to + tile], sems.at[len(copies)])
            )
            copies[-1].start()
    for copy in copies:
        copy.wait()


def tiles(made, total, place):
    edges = set(range(0, made, TILE)) | {made}
    if place is not None and place + made > total:
        edges = set(range(0, total - place, TILE)) | set(range(total - place, made, TILE)) | {made}
    edges = sorted(edges)
    return [(lo, hi - lo) for lo, hi in zip(edges[:-1], edges[1:])]


def layer_chunk(bands, weights, chunk, prev, first_chunk, first, last, place=None, whole=None):
    own = chunk[0]
    rows, width, channels = own.shape
    made = width + (0 if first else PAD) + (0 if last else -PAD) + (PAD if last else 0) - (PAD if first else 0)
    window = made + 2 * PAD
    args = list(weights) + list(chunk)
    if not first:
        args += list(prev)
    if last and not first:
        args += list(first_chunk)
    specs = [pl.BlockSpec(memory_space=pltpu.VMEM)] * len(args)
    strip = jax.ShapeDtypeStruct((rows, 2 * PAD, channels), jnp.bfloat16)
    outs = [jax.ShapeDtypeStruct((rows, made, channels), jnp.bfloat16)]
    out_specs = [pl.BlockSpec(memory_space=pltpu.VMEM)]
    scratch = [
        pltpu.VMEM((rows, window, channels), jnp.float32),
        pltpu.VMEM((rows, window, channels), jnp.bfloat16),
    ]
    aliases = {}
    if place is not None:
        lons = whole if first else whole.shape[1]
        scratch += [pltpu.VMEM(outs[0].shape, jnp.bfloat16), pltpu.SemaphoreType.DMA((len(tiles(made, lons, place)),))]
        outs = [jax.ShapeDtypeStruct((rows, lons, channels), jnp.bfloat16)]
        out_specs = [pl.BlockSpec(memory_space=pltpu.HBM)]
        if not first:
            aliases = {len(args): 0}
            args.append(whole)
            specs += out_specs
    if not last:
        outs.append(strip)
    if first and not last:
        outs.append(strip)
    out_specs += [pl.BlockSpec(memory_space=pltpu.VMEM)] * (len(outs) - 1)
    cells = rows * made
    hidden = weights[3].shape[1]
    return pl.pallas_call(
        functools.partial(chunk_kernel, bands, first, last, width, place),
        out_shape=outs,
        in_specs=specs,
        out_specs=out_specs,
        scratch_shapes=scratch,
        input_output_aliases=aliases,
        compiler_params=pltpu.CompilerParams(vmem_limit_bytes=24 * 2**20),
        cost_estimate=pl.CostEstimate(
            flops=50 * cells * channels * hidden, bytes_accessed=8 * cells * channels, transcendentals=cells * hidden
        ),
    )(*args)


def splits(total):
    tiles = total // PAD
    edges = [0, PAD * (11 * tiles // 36), PAD * (24 * tiles // 36), total]
    return list(zip(edges[:-1], edges[1:]))


def swaps(bands, start):
    return [pair for b in range(start, bands - 1, 2) for pair in ((b, b + 1), (b + 1, b))]


def member_step(state, weights, bands):
    rows, lons, _ = state.shape
    assert rows == REACH
    even_pairs, odd_pairs = swaps(bands, 0), swaps(bands, 1)
    ranges = splits(lons)
    chunks, sums = [first_columns(state, ranges[0][1])], []
    sums.append(own_share(weights[0][0], chunks[0], 0, ranges[0][1], [])[0])
    for lo, hi in ranges[1:]:
        share, copy = own_share(weights[0][0], state, lo, hi, sums[-1:])
        sums.append(share)
        chunks.append(copy)
    whole, place = lons, LAYERS * PAD
    for layer in range(LAYERS):
        halos = [(lax.ppermute(own, "band", even_pairs), lax.ppermute(own, "band", odd_pairs)) for own in chunks]
        if layer > 0:
            sums = [own_share(weights[layer][0], own, 0, own.shape[1], [])[0] for own in chunks]
        final = layer == LAYERS - 1
        made, prev, first_chunk = [], None, None
        for c, own in enumerate(chunks):
            first, last = c == 0, c == len(chunks) - 1
            where = (place, whole) if final else ()
            got = layer_chunk(bands, weights[layer], (own, sums[c]) + halos[c], prev, first_chunk, first, last, *where)
            made.append(got[0])
            if final:
                whole = got[0]
                place += own.shape[1] - (2 * PAD if first else 0)
            if not last:
                prev = (own, got[1])
            if first and not last:
                first_chunk = (own[:, : 2 * PAD], got[2])
        chunks = made
    return whole


def solution(mesh):
    bands = mesh.shape["band"]

    def shards(fields, lat_taps, lon_taps, gains, w_in, w_out):
        weights = [
            (
                lat_taps[layer].astype(jnp.float32),
                lon_taps[layer].astype(jnp.float32),
                gains[layer : layer + 1],
                w_in[layer],
                w_out[layer],
            )
            for layer in range(LAYERS)
        ]
        return jnp.concatenate([member_step(fields[m], weights, bands)[None] for m in range(fields.shape[0])])

    return jax.shard_map(
        shards,
        mesh=mesh,
        in_specs=(P(("members", "section"), "band", None, None), P(), P(), P(), P(), P()),
        out_specs=P(("members", "section"), "band", None, None),
        check_vma=False,
    )
```

```python
import functools

import jax
import jax.numpy as jnp
from jax import lax
from jax.experimental import pallas as pl
from jax.experimental.pallas import tpu as pltpu
from jax.sharding import PartitionSpec as P

DLON = 3
LAYERS = 2
TAPS = 9
REACH = TAPS // 2
PAD = 16
TILE = 32


def gelu(x):
    return 0.5 * x * (1.0 + lax.erf(x * 0.7071067811865476))


def copy_kernel(lo, state, *refs):
    out = refs[-1]
    out[...] = state[:, lo : lo + out.shape[1]]


def later_columns(state, lo, hi, after):
    rows, _, channels = state.shape
    return pl.pallas_call(
        functools.partial(copy_kernel, lo),
        out_shape=jax.ShapeDtypeStruct((rows, hi - lo, channels), state.dtype),
        in_specs=[pl.BlockSpec(memory_space=pltpu.VMEM)] + [pl.BlockSpec(memory_space=pl.ANY)] * len(after),
        out_specs=pl.BlockSpec(memory_space=pltpu.VMEM),
        compiler_params=pltpu.CompilerParams(vmem_limit_bytes=16 * 2**20),
        cost_estimate=pl.CostEstimate(flops=2 * 10**9, bytes_accessed=4 * rows * (hi - lo) * channels, transcendentals=0),
    )(state, *after)


def chunk_kernel(bands, first, last, width, place, *refs):
    refs = list(refs)
    lat_w, lon_w, gain, w_in, w_out, own, odd_swap, even_swap = refs[:8]
    refs = refs[8:]
    if not first:
        prev_own, prev_mix = refs[:2]
        refs = refs[2:]
    if last and not first:
        first_own, first_mix = refs[:2]
        refs = refs[2:]
    if place is not None and not first:
        refs.pop(0)
    out = refs.pop(0)
    if not last:
        tail = refs.pop(0)
    if first and not last:
        head = refs.pop(0)
    mix, state = refs[:2]
    whole = out
    if place is not None:
        out, sems = refs[2:]
    rows = own.shape[0]
    channels = own.shape[2]
    start = 0 if first else 2 * PAD

    if not first:
        mix[:, : 2 * PAD] = prev_mix[...].astype(jnp.float32)
        state[:, : 2 * PAD] = prev_own[:, prev_own.shape[1] - 2 * PAD :]
    if last and not first:
        mix[:, start + width :] = first_mix[...].astype(jnp.float32)
        state[:, start + width :] = first_own[:, : 2 * PAD]

    band = lax.axis_index("band")
    is_odd = lax.rem(band, 2) == 1
    lat_tap = [jnp.broadcast_to(lat_w[k : k + 1], (PAD, channels)) for k in range(TAPS)]

    def mix_tile(t, carry):
        at = pl.multiple_of(t * PAD, PAD)
        to = pl.multiple_of(start + t * PAD, PAD)
        evens = [even_swap[r, pl.ds(at, PAD)] for r in range(REACH)]
        odds = [odd_swap[r, pl.ds(at, PAD)] for r in range(REACH)]
        above = [jnp.where(is_odd, e, o) for e, o in zip(evens, odds)]
        below = [jnp.where(is_odd, o, e) for e, o in zip(evens, odds)]
        mine = [own[r, pl.ds(at, PAD)] for r in range(rows)]
        strip = [s.astype(jnp.float32) for s in above + mine + below]
        for r in range(rows):
            total = strip[r] * lat_tap[0]
            for k in range(1, TAPS):
                total = total + strip[r + k] * lat_tap[k]
            mix[r, pl.ds(to, PAD)] = total.astype(jnp.bfloat16).astype(jnp.float32)
            state[r, pl.ds(to, PAD)] = mine[r]
        return carry

    lax.fori_loop(0, width // PAD, mix_tile, 0)

    if not last:
        tail[...] = mix[:, start + width - 2 * PAD : start + width].astype(jnp.bfloat16)
    if first and not last:
        head[...] = mix[:, : 2 * PAD].astype(jnp.bfloat16)
    if first and last:
        mix[:, width:] = mix[:, : 2 * PAD]
        state[:, width:] = state[:, : 2 * PAD]

    lon_tap = [lon_w[k : k + 1] for k in range(TAPS)]
    scale = gain[...]
    made, total = out.shape[1], whole.shape[1]

    def rest(at, tile):
        parts = []
        for r in range(rows):
            lon = mix[r, pl.ds(at + PAD - DLON * REACH, tile)] * lon_tap[0]
            for k in range(1, TAPS):
                lon = lon + mix[r, pl.ds(at + PAD + DLON * (k - REACH), tile)] * lon_tap[k]
            parts.append(lon)
        lon = jnp.concatenate(parts, axis=0)
        mean = jnp.mean(lon, axis=-1, keepdims=True)
        centred = lon - mean
        var = jnp.mean(centred * centred, axis=-1, keepdims=True)
        normed = (centred * lax.rsqrt(var + 1e-06) * scale).astype(jnp.bfloat16)
        hidden = jnp.dot(normed, w_in[...], preferred_element_type=jnp.float32)
        hidden = gelu(hidden).astype(jnp.bfloat16)
        delta = jnp.dot(hidden, w_out[...], preferred_element_type=jnp.float32)
        for r in range(rows):
            new = state[r, pl.ds(at + PAD, tile)].astype(jnp.float32) + delta[r * tile : (r + 1) * tile]
            out[r, pl.ds(at, tile)] = new.astype(jnp.bfloat16)

    copies = []
    for at, tile in tiles(made, total, place):
        rest(at, tile)
        if place is not None:
            to = (place + at) % total
            copies.append(
                pltpu.make_async_copy(out.at[:, at : at + tile], whole.at[:, to : to + tile], sems.at[len(copies)])
            )
            copies[-1].start()
    for copy in copies:
        copy.wait()


def tiles(made, total, place):
    edges = set(range(0, made, TILE)) | {made}
    if place is not None and place + made > total:
        edges = set(range(0, total - place, TILE)) | set(range(total - place, made, TILE)) | {made}
    edges = sorted(edges)
    return [(lo, hi - lo) for lo, hi in zip(edges[:-1], edges[1:])]


def layer_chunk(bands, weights, chunk, prev, first_chunk, first, last, place=None, whole=None):
    own = chunk[0]
    rows, width, channels = own.shape
    made = width + (0 if first else PAD) + (0 if last else -PAD) + (PAD if last else 0) - (PAD if first else 0)
    window = made + 2 * PAD
    args = list(weights) + list(chunk)
    if not first:
        args += list(prev)
    if last and not first:
        args += list(first_chunk)
    specs = [pl.BlockSpec(memory_space=pltpu.VMEM)] * len(args)
    strip = jax.ShapeDtypeStruct((rows, 2 * PAD, channels), jnp.bfloat16)
    outs = [jax.ShapeDtypeStruct((rows, made, channels), jnp.bfloat16)]
    out_specs = [pl.BlockSpec(memory_space=pltpu.VMEM)]
    scratch = [
        pltpu.VMEM((rows, window, channels), jnp.float32),
        pltpu.VMEM((rows, window, channels), jnp.bfloat16),
    ]
    aliases = {}
    if place is not None:
        lons = whole if first else whole.shape[1]
        scratch += [pltpu.VMEM(outs[0].shape, jnp.bfloat16), pltpu.SemaphoreType.DMA((len(tiles(made, lons, place)),))]
        outs = [jax.ShapeDtypeStruct((rows, lons, channels), jnp.bfloat16)]
        out_specs = [pl.BlockSpec(memory_space=pltpu.HBM)]
        if not first:
            aliases = {len(args): 0}
            args.append(whole)
            specs += out_specs
    if not last:
        outs.append(strip)
    if first and not last:
        outs.append(strip)
    out_specs += [pl.BlockSpec(memory_space=pltpu.VMEM)] * (len(outs) - 1)
    cells = rows * made
    hidden = weights[3].shape[1]
    return pl.pallas_call(
        functools.partial(chunk_kernel, bands, first, last, width, place),
        out_shape=outs,
        in_specs=specs,
        out_specs=out_specs,
        scratch_shapes=scratch,
        input_output_aliases=aliases,
        compiler_params=pltpu.CompilerParams(vmem_limit_bytes=24 * 2**20),
        cost_estimate=pl.CostEstimate(
            flops=50 * cells * channels * hidden, bytes_accessed=8 * cells * channels, transcendentals=cells * hidden
        ),
    )(*args)


def splits(total):
    first = PAD * ((total // PAD + 2 * LAYERS) // 2)
    return [(0, first), (first, total)]


def swaps(bands, start):
    return [pair for b in range(start, bands - 1, 2) for pair in ((b, b + 1), (b + 1, b))]


def member_step(state, weights, bands):
    rows, lons, _ = state.shape
    assert rows == REACH
    even_pairs, odd_pairs = swaps(bands, 0), swaps(bands, 1)
    ranges = splits(lons)
    chunks = [state[:, : ranges[0][1]]]
    ready = [w for layer_weights in weights for w in layer_weights]
    for lo, hi in ranges[1:]:
        chunks.append(later_columns(state, lo, hi, ready))
    whole, place = lons, LAYERS * PAD
    for layer in range(LAYERS):
        halos = []
        for own in chunks:
            odd_swap = lax.ppermute(own, "band", odd_pairs)
            even_swap = lax.ppermute(own, "band", even_pairs)
            halos.append((odd_swap, even_swap))
        final = layer == LAYERS - 1
        made, prev, first_chunk = [], None, None
        for c, own in enumerate(chunks):
            first, last = c == 0, c == len(chunks) - 1
            where = (place, whole) if final else ()
            got = layer_chunk(bands, weights[layer], (own,) + halos[c], prev, first_chunk, first, last, *where)
            made.append(got[0])
            if final:
                whole = got[0]
                place += own.shape[1] - (2 * PAD if first else 0)
            if not last:
                prev = (own, got[1])
            if first and not last:
                first_chunk = (own[:, : 2 * PAD], got[2])
        chunks = made
    return whole


def solution(mesh):
    bands = mesh.shape["band"]

    def shards(fields, lat_taps, lon_taps, gains, w_in, w_out):
        weights = [
            (
                lat_taps[layer].astype(jnp.float32),
                lon_taps[layer].astype(jnp.float32),
                gains[layer : layer + 1],
                w_in[layer],
                w_out[layer],
            )
            for layer in range(LAYERS)
        ]
        return jnp.concatenate([member_step(fields[m], weights, bands)[None] for m in range(fields.shape[0])])

    return jax.shard_map(
        shards,
        mesh=mesh,
        in_specs=(P(("members", "section"), "band", None, None), P(), P(), P(), P(), P()),
        out_specs=P(("members", "section"), "band", None, None),
        check_vma=False,
    )
```

```python
import functools

import jax
import jax.numpy as jnp
from jax import lax
from jax.experimental import pallas as pl
from jax.experimental.pallas import tpu as pltpu
from jax.sharding import PartitionSpec as P

DLON = 3
LAYERS = 2
TAPS = 9
REACH = TAPS // 2
PAD = 16
TILE = 32


def gelu(x):
    return 0.5 * x * (1.0 + lax.erf(x * 0.7071067811865476))


def copy_kernel(lo, state, *refs):
    out = refs[-1]
    out[...] = state[:, lo : lo + out.shape[1]]


def later_columns(state, lo, hi, after):
    rows, _, channels = state.shape
    return pl.pallas_call(
        functools.partial(copy_kernel, lo),
        out_shape=jax.ShapeDtypeStruct((rows, hi - lo, channels), state.dtype),
        in_specs=[pl.BlockSpec(memory_space=pltpu.VMEM)] + [pl.BlockSpec(memory_space=pl.ANY)] * len(after),
        out_specs=pl.BlockSpec(memory_space=pltpu.VMEM),
        compiler_params=pltpu.CompilerParams(vmem_limit_bytes=16 * 2**20),
        cost_estimate=pl.CostEstimate(flops=2 * 10**9, bytes_accessed=4 * rows * (hi - lo) * channels, transcendentals=0),
    )(state, *after)


def chunk_kernel(layer, first, last, width, place, *refs):
    refs = list(refs)
    lat_w, lon_w, gain, w_in, w_out, own, odd_swap, even_swap = refs[:8]
    refs = refs[8:]
    if not first:
        prev_own, prev_mix = refs[:2]
        refs = refs[2:]
    if last and not first:
        first_own, first_mix = refs[:2]
        refs = refs[2:]
    if place is not None and not first:
        refs.pop(0)
    out = refs.pop(0)
    if not last:
        tail = refs.pop(0)
    if first and not last:
        head = refs.pop(0)
    mix, state = refs[:2]
    whole = out
    if place is not None:
        out, sems = refs[2:]
    rows = own.shape[0]
    channels = own.shape[2]
    start = 0 if first else 2 * PAD

    if not first:
        mix[:, : 2 * PAD] = prev_mix[...].astype(jnp.float32)
        state[:, : 2 * PAD] = prev_own[:, prev_own.shape[1] - 2 * PAD :]
    if last and not first:
        mix[:, start + width :] = first_mix[...].astype(jnp.float32)
        state[:, start + width :] = first_own[:, : 2 * PAD]

    band = lax.axis_index("band")
    is_odd = lax.rem(band, 2) == 1
    lat_rows = lat_w[...].astype(jnp.float32)
    lat_tap = [jnp.broadcast_to(lat_rows[k, layer : layer + 1], (PAD, channels)) for k in range(TAPS)]

    def mix_tile(t, carry):
        at = pl.multiple_of(t * PAD, PAD)
        to = pl.multiple_of(start + t * PAD, PAD)
        evens = [even_swap[r, pl.ds(at, PAD)] for r in range(REACH)]
        odds = [odd_swap[r, pl.ds(at, PAD)] for r in range(REACH)]
        above = [jnp.where(is_odd, e, o) for e, o in zip(evens, odds)]
        below = [jnp.where(is_odd, o, e) for e, o in zip(evens, odds)]
        mine = [own[r, pl.ds(at, PAD)] for r in range(rows)]
        strip = [s.astype(jnp.float32) for s in above + mine + below]
        for r in range(rows):
            total = strip[r] * lat_tap[0]
            for k in range(1, TAPS):
                total = total + strip[r + k] * lat_tap[k]
            mix[r, pl.ds(to, PAD)] = total.astype(jnp.bfloat16).astype(jnp.float32)
            state[r, pl.ds(to, PAD)] = mine[r]
        return carry

    lax.fori_loop(0, width // PAD, mix_tile, 0)

    if not last:
        tail[...] = mix[:, start + width - 2 * PAD : start + width].astype(jnp.bfloat16)
    if first and not last:
        head[...] = mix[:, : 2 * PAD].astype(jnp.bfloat16)
    if first and last:
        mix[:, width:] = mix[:, : 2 * PAD]
        state[:, width:] = state[:, : 2 * PAD]

    lon_rows = lon_w[...].astype(jnp.float32)
    lon_tap = [lon_rows[k, layer : layer + 1] for k in range(TAPS)]
    scale = gain[layer : layer + 1]
    made, total = out.shape[1], whole.shape[1]

    def rest(at, tile):
        parts = []
        for r in range(rows):
            lon = mix[r, pl.ds(at + PAD - DLON * REACH, tile)] * lon_tap[0]
            for k in range(1, TAPS):
                lon = lon + mix[r, pl.ds(at + PAD + DLON * (k - REACH), tile)] * lon_tap[k]
            parts.append(lon)
        lon = jnp.concatenate(parts, axis=0)
        mean = jnp.mean(lon, axis=-1, keepdims=True)
        centred = lon - mean
        var = jnp.mean(centred * centred, axis=-1, keepdims=True)
        normed = (centred * lax.rsqrt(var + 1e-06) * scale).astype(jnp.bfloat16)
        hidden = jnp.dot(normed, w_in[layer], preferred_element_type=jnp.float32)
        hidden = gelu(hidden).astype(jnp.bfloat16)
        delta = jnp.dot(hidden, w_out[layer], preferred_element_type=jnp.float32)
        for r in range(rows):
            new = state[r, pl.ds(at + PAD, tile)].astype(jnp.float32) + delta[r * tile : (r + 1) * tile]
            out[r, pl.ds(at, tile)] = new.astype(jnp.bfloat16)

    copies = []
    for at, tile in tiles(made, total, place):
        rest(at, tile)
        if place is not None:
            to = (place + at) % total
            copies.append(
                pltpu.make_async_copy(out.at[:, at : at + tile], whole.at[:, to : to + tile], sems.at[len(copies)])
            )
            copies[-1].start()
    for copy in copies:
        copy.wait()


def tiles(made, total, place):
    edges = set(range(0, made, TILE)) | {made}
    if place is not None and place + made > total:
        edges = set(range(0, total - place, TILE)) | set(range(total - place, made, TILE)) | {made}
    edges = sorted(edges)
    return [(lo, hi - lo) for lo, hi in zip(edges[:-1], edges[1:])]


def layer_chunk(layer, weights, chunk, prev, first_chunk, first, last, place=None, whole=None):
    own = chunk[0]
    rows, width, channels = own.shape
    made = width + (0 if first else PAD) + (0 if last else -PAD) + (PAD if last else 0) - (PAD if first else 0)
    window = made + 2 * PAD
    args = list(weights) + list(chunk)
    if not first:
        args += list(prev)
    if last and not first:
        args += list(first_chunk)
    specs = [pl.BlockSpec(memory_space=pltpu.VMEM)] * len(args)
    strip = jax.ShapeDtypeStruct((rows, 2 * PAD, channels), jnp.bfloat16)
    outs = [jax.ShapeDtypeStruct((rows, made, channels), jnp.bfloat16)]
    out_specs = [pl.BlockSpec(memory_space=pltpu.VMEM)]
    scratch = [
        pltpu.VMEM((rows, window, channels), jnp.float32),
        pltpu.VMEM((rows, window, channels), jnp.bfloat16),
    ]
    aliases = {}
    if place is not None:
        lons = whole if first else whole.shape[1]
        scratch += [pltpu.VMEM(outs[0].shape, jnp.bfloat16), pltpu.SemaphoreType.DMA((len(tiles(made, lons, place)),))]
        outs = [jax.ShapeDtypeStruct((rows, lons, channels), jnp.bfloat16)]
        out_specs = [pl.BlockSpec(memory_space=pltpu.HBM)]
        if not first:
            aliases = {len(args): 0}
            args.append(whole)
            specs += out_specs
    if not last:
        outs.append(strip)
    if first and not last:
        outs.append(strip)
    out_specs += [pl.BlockSpec(memory_space=pltpu.VMEM)] * (len(outs) - 1)
    cells = rows * made
    hidden = weights[3].shape[2]
    return pl.pallas_call(
        functools.partial(chunk_kernel, layer, first, last, width, place),
        out_shape=outs,
        in_specs=specs,
        out_specs=out_specs,
        scratch_shapes=scratch,
        input_output_aliases=aliases,
        compiler_params=pltpu.CompilerParams(vmem_limit_bytes=24 * 2**20),
        cost_estimate=pl.CostEstimate(
            flops=50 * cells * channels * hidden, bytes_accessed=8 * cells * channels, transcendentals=cells * hidden
        ),
    )(*args)


def splits(total):
    tiles = total // PAD
    edges = [0, PAD * (11 * tiles // 36), PAD * (24 * tiles // 36), total]
    return list(zip(edges[:-1], edges[1:]))


def swaps(bands, start):
    return [pair for b in range(start, bands - 1, 2) for pair in ((b, b + 1), (b + 1, b))]


def member_step(state, weights, bands):
    rows, lons, _ = state.shape
    assert rows == REACH
    even_pairs, odd_pairs = swaps(bands, 0), swaps(bands, 1)
    ranges = splits(lons)
    chunks = [state[:, : ranges[0][1]]]
    for lo, hi in ranges[1:]:
        chunks.append(later_columns(state, lo, hi, chunks[1:][-1:]))
    whole, place = lons, LAYERS * PAD
    for layer in range(LAYERS):
        halos = []
        for own in chunks:
            odd_swap = lax.ppermute(own, "band", odd_pairs)
            even_swap = lax.ppermute(own, "band", even_pairs)
            halos.append((odd_swap, even_swap))
        final = layer == LAYERS - 1
        made, prev, first_chunk = [], None, None
        for c, own in enumerate(chunks):
            first, last = c == 0, c == len(chunks) - 1
            where = (place, whole) if final else ()
            got = layer_chunk(layer, weights, (own,) + halos[c], prev, first_chunk, first, last, *where)
            made.append(got[0])
            if final:
                whole = got[0]
                place += own.shape[1] - (2 * PAD if first else 0)
            if not last:
                prev = (own, got[1])
            if first and not last:
                first_chunk = (own, got[2])
        chunks = made
    return whole


def solution(mesh):
    bands = mesh.shape["band"]

    def shards(fields, lat_taps, lon_taps, gains, w_in, w_out):
        weights = (lat_taps.transpose(1, 0, 2), lon_taps.transpose(1, 0, 2), gains, w_in, w_out)
        return jnp.concatenate([member_step(fields[m], weights, bands)[None] for m in range(fields.shape[0])])

    return jax.shard_map(
        shards,
        mesh=mesh,
        in_specs=(P(("members", "section"), "band", None, None), P(), P(), P(), P(), P()),
        out_specs=P(("members", "section"), "band", None, None),
        check_vma=False,
    )
```

```python
import functools

import jax
import jax.numpy as jnp
from jax import lax
from jax.experimental import pallas as pl
from jax.experimental.pallas import tpu as pltpu
from jax.sharding import PartitionSpec as P

DLON = 3
LAYERS = 2
TAPS = 9
REACH = TAPS // 2
PAD = 16
TILE = 96
SEGMENTS = 8
GROUP = 16


def gelu(x):
    return 0.5 * x * (1.0 + lax.erf(x * 0.7071067811865476))


def copy_kernel(lo, state, *refs):
    out = refs[-1]
    out[...] = state[:, lo : lo + out.shape[1]]


def later_columns(state, lo, hi, after):
    rows, _, channels = state.shape
    return pl.pallas_call(
        functools.partial(copy_kernel, lo),
        out_shape=jax.ShapeDtypeStruct((rows, hi - lo, channels), state.dtype),
        in_specs=[pl.BlockSpec(memory_space=pltpu.VMEM)] + [pl.BlockSpec(memory_space=pl.ANY)] * len(after),
        out_specs=pl.BlockSpec(memory_space=pltpu.VMEM),
        compiler_params=pltpu.CompilerParams(vmem_limit_bytes=16 * 2**20),
        cost_estimate=pl.CostEstimate(flops=2 * 10**9, bytes_accessed=4 * rows * (hi - lo) * channels, transcendentals=0),
    )(state, *after)


def chunk_kernel(layer, first, last, width, place, *refs):
    refs = list(refs)
    lat_w, lon_w, gain, w_in, w_out, own, odd_swap, even_swap = refs[:8]
    refs = refs[8:]
    if not first:
        prev_own, prev_mix = refs[:2]
        refs = refs[2:]
    if last and not first:
        first_own, first_mix = refs[:2]
        refs = refs[2:]
    if place is not None and not first:
        refs.pop(0)
    out = refs.pop(0)
    if not last:
        tail = refs.pop(0)
    if first and not last:
        head = refs.pop(0)
    mix, state, deltas = refs[:3]
    whole = out
    if place is not None:
        out, sems = refs[3:]
    rows = own.shape[0]
    channels = own.shape[2]
    start = 0 if first else 2 * PAD

    if not first:
        mix[:, : 2 * PAD] = prev_mix[...].astype(jnp.float32)
        state[:, : 2 * PAD] = prev_own[:, prev_own.shape[1] - 2 * PAD :]
    if last and not first:
        mix[:, start + width : start + width + 2 * PAD] = first_mix[...].astype(jnp.float32)
        state[:, start + width :] = first_own[:, : 2 * PAD]

    band = lax.axis_index("band")
    is_odd = lax.rem(band, 2) == 1
    lat_rows = lat_w[...].astype(jnp.float32)
    lat_tap = [jnp.broadcast_to(lat_rows[k, layer : layer + 1], (PAD, channels)) for k in range(TAPS)]

    def mix_tile(t, carry):
        at = pl.multiple_of(t * PAD, PAD)
        to = pl.multiple_of(start + t * PAD, PAD)
        evens = [even_swap[r, pl.ds(at, PAD)] for r in range(REACH)]
        odds = [odd_swap[r, pl.ds(at, PAD)] for r in range(REACH)]
        above = [jnp.where(is_odd, e, o) for e, o in zip(evens, odds)]
        below = [jnp.where(is_odd, o, e) for e, o in zip(evens, odds)]
        mine = [own[r, pl.ds(at, PAD)] for r in range(rows)]
        strip = [s.astype(jnp.float32) for s in above + mine + below]
        for r in range(rows):
            total = strip[r] * lat_tap[0]
            for k in range(1, TAPS):
                total = total + strip[r + k] * lat_tap[k]
            mix[r, pl.ds(to, PAD)] = total.astype(jnp.bfloat16).astype(jnp.float32)
            state[r, pl.ds(to, PAD)] = mine[r]
        return carry

    lax.fori_loop(0, width // PAD, mix_tile, 0)

    if not last:
        tail[...] = mix[:, start + width - 2 * PAD : start + width].astype(jnp.bfloat16)
    if first and not last:
        head[...] = mix[:, : 2 * PAD].astype(jnp.bfloat16)
    if first and last:
        mix[:, width : width + 2 * PAD] = mix[:, : 2 * PAD]
        state[:, width:] = state[:, : 2 * PAD]

    lon_rows = lon_w[...].astype(jnp.float32)
    lon_tap = [lon_rows[k, layer : layer + 1] for k in range(TAPS)]
    scale = gain[layer : layer + 1]
    made, total = out.shape[1], whole.shape[1]

    stride = segment(made)
    spare = mix.shape[1] - made - 2 * PAD
    if spare:
        mix[:, made + 2 * PAD :] = jnp.zeros((rows, spare, channels), jnp.float32)
    group = []

    def mlp():
        lon = jnp.concatenate([x for _, _, x in group], axis=0)
        mean = jnp.mean(lon, axis=-1, keepdims=True)
        centred = lon - mean
        var = jnp.mean(centred * centred, axis=-1, keepdims=True)
        normed = (centred * lax.rsqrt(var + 1e-06) * scale).astype(jnp.bfloat16)
        hidden = jnp.dot(normed, w_in[layer], preferred_element_type=jnp.float32)
        hidden = gelu(hidden).astype(jnp.bfloat16)
        delta = jnp.dot(hidden, w_out[layer], preferred_element_type=jnp.float32)
        for i, (r, m, _) in enumerate(group):
            deltas[r, pl.ds(m, SEGMENTS, stride=stride)] = delta[i * SEGMENTS : (i + 1) * SEGMENTS]
        group.clear()

    for r in range(rows):
        held = {}
        for m in range(stride):
            lon = None
            for k in range(TAPS):
                at = m + DLON * k
                if at not in held:
                    held[at] = mix[r, pl.ds(at + PAD - DLON * REACH, SEGMENTS, stride=stride)]
                term = held[at] * lon_tap[k]
                lon = term if lon is None else lon + term
            del held[m]
            group.append((r, m, lon))
            if len(group) == GROUP:
                mlp()
    if group:
        mlp()

    def rest(at, tile):
        for r in range(rows):
            new = state[r, at + PAD : at + PAD + tile].astype(jnp.float32) + deltas[r, at : at + tile]
            out[r, at : at + tile] = new.astype(jnp.bfloat16)

    copies = []
    for at, tile in tiles(made, total, place):
        rest(at, tile)
        if place is not None:
            to = (place + at) % total
            copies.append(
                pltpu.make_async_copy(out.at[:, at : at + tile], whole.at[:, to : to + tile], sems.at[len(copies)])
            )
            copies[-1].start()
    for copy in copies:
        copy.wait()


def segment(made):
    return (made + SEGMENTS - 1) // SEGMENTS | 1


def tiles(made, total, place):
    edges = set(range(0, made, TILE)) | {made}
    if place is not None and place + made > total:
        edges = set(range(0, total - place, TILE)) | set(range(total - place, made, TILE)) | {made}
    edges = sorted(edges)
    return [(lo, hi - lo) for lo, hi in zip(edges[:-1], edges[1:])]


def layer_chunk(layer, weights, chunk, prev, first_chunk, first, last, place=None, whole=None):
    own = chunk[0]
    rows, width, channels = own.shape
    made = width + (0 if first else PAD) + (0 if last else -PAD) + (PAD if last else 0) - (PAD if first else 0)
    window = made + 2 * PAD
    args = list(weights) + list(chunk)
    if not first:
        args += list(prev)
    if last and not first:
        args += list(first_chunk)
    specs = [pl.BlockSpec(memory_space=pltpu.VMEM)] * len(args)
    strip = jax.ShapeDtypeStruct((rows, 2 * PAD, channels), jnp.bfloat16)
    outs = [jax.ShapeDtypeStruct((rows, made, channels), jnp.bfloat16)]
    out_specs = [pl.BlockSpec(memory_space=pltpu.VMEM)]
    scratch = [
        pltpu.VMEM((rows, SEGMENTS * segment(made) + 2 * PAD, channels), jnp.float32),
        pltpu.VMEM((rows, window, channels), jnp.bfloat16),
        pltpu.VMEM((rows, SEGMENTS * segment(made), channels), jnp.float32),
    ]
    aliases = {}
    if place is not None:
        lons = whole if first else whole.shape[1]
        scratch += [pltpu.VMEM(outs[0].shape, jnp.bfloat16), pltpu.SemaphoreType.DMA((len(tiles(made, lons, place)),))]
        outs = [jax.ShapeDtypeStruct((rows, lons, channels), jnp.bfloat16)]
        out_specs = [pl.BlockSpec(memory_space=pltpu.HBM)]
        if not first:
            aliases = {len(args): 0}
            args.append(whole)
            specs += out_specs
    if not last:
        outs.append(strip)
    if first and not last:
        outs.append(strip)
    out_specs += [pl.BlockSpec(memory_space=pltpu.VMEM)] * (len(outs) - 1)
    cells = rows * made
    hidden = weights[3].shape[2]
    return pl.pallas_call(
        functools.partial(chunk_kernel, layer, first, last, width, place),
        out_shape=outs,
        in_specs=specs,
        out_specs=out_specs,
        scratch_shapes=scratch,
        input_output_aliases=aliases,
        compiler_params=pltpu.CompilerParams(vmem_limit_bytes=24 * 2**20),
        cost_estimate=pl.CostEstimate(
            flops=50 * cells * channels * hidden, bytes_accessed=8 * cells * channels, transcendentals=cells * hidden
        ),
    )(*args)


def splits(total):
    tiles = total // PAD
    edges = [0, PAD * (11 * tiles // 36), PAD * (24 * tiles // 36), total]
    return list(zip(edges[:-1], edges[1:]))


def swaps(bands, start):
    return [pair for b in range(start, bands - 1, 2) for pair in ((b, b + 1), (b + 1, b))]


def member_step(state, weights, bands):
    rows, lons, _ = state.shape
    assert rows == REACH
    even_pairs, odd_pairs = swaps(bands, 0), swaps(bands, 1)
    ranges = splits(lons)
    chunks = [state[:, : ranges[0][1]]]
    for lo, hi in ranges[1:]:
        chunks.append(later_columns(state, lo, hi, chunks[1:][-1:]))
    whole, place = lons, LAYERS * PAD
    for layer in range(LAYERS):
        halos = []
        for own in chunks:
            odd_swap = lax.ppermute(own, "band", odd_pairs)
            even_swap = lax.ppermute(own, "band", even_pairs)
            halos.append((odd_swap, even_swap))
        final = layer == LAYERS - 1
        made, prev, first_chunk = [], None, None
        for c, own in enumerate(chunks):
            first, last = c == 0, c == len(chunks) - 1
            where = (place, whole) if final else ()
            got = layer_chunk(layer, weights, (own,) + halos[c], prev, first_chunk, first, last, *where)
            made.append(got[0])
            if final:
                whole = got[0]
                place += own.shape[1] - (2 * PAD if first else 0)
            if not last:
                prev = (own, got[1])
            if first and not last:
                first_chunk = (own, got[2])
        chunks = made
    return whole


def solution(mesh):
    bands = mesh.shape["band"]

    def shards(fields, lat_taps, lon_taps, gains, w_in, w_out):
        weights = (lat_taps.transpose(1, 0, 2), lon_taps.transpose(1, 0, 2), gains, w_in, w_out)
        return jnp.concatenate([member_step(fields[m], weights, bands)[None] for m in range(fields.shape[0])])

    return jax.shard_map(
        shards,
        mesh=mesh,
        in_specs=(P(("members", "section"), "band", None, None), P(), P(), P(), P(), P()),
        out_specs=P(("members", "section"), "band", None, None),
        check_vma=False,
    )
```

```python
import functools

import jax
import jax.numpy as jnp
from jax import lax
from jax.experimental import pallas as pl
from jax.experimental.pallas import tpu as pltpu
from jax.sharding import PartitionSpec as P

DLON = 3
LAYERS = 2
TAPS = 9
REACH = TAPS // 2
PAD = 16
TILE = 32


def gelu(x):
    return 0.5 * x * (1.0 + lax.erf(x * 0.7071067811865476))


def copy_kernel(lo, state, *refs):
    out = refs[-1]
    out[...] = state[:, lo : lo + out.shape[1]]


def later_columns(state, lo, hi, after):
    rows, _, channels = state.shape
    return pl.pallas_call(
        functools.partial(copy_kernel, lo),
        out_shape=jax.ShapeDtypeStruct((rows, hi - lo, channels), state.dtype),
        in_specs=[pl.BlockSpec(memory_space=pltpu.VMEM)] + [pl.BlockSpec(memory_space=pl.ANY)] * len(after),
        out_specs=pl.BlockSpec(memory_space=pltpu.VMEM),
        compiler_params=pltpu.CompilerParams(vmem_limit_bytes=16 * 2**20),
        cost_estimate=pl.CostEstimate(flops=2 * 10**9, bytes_accessed=4 * rows * (hi - lo) * channels, transcendentals=0),
    )(state, *after)


def chunk_kernel(layer, first, last, width, place, *refs):
    refs = list(refs)
    lat_w, lon_w, gain, w_in, w_out, own, odd_swap, even_swap = refs[:8]
    refs = refs[8:]
    if not first:
        prev_own, prev_mix = refs[:2]
        refs = refs[2:]
    if last and not first:
        first_own, first_mix = refs[:2]
        refs = refs[2:]
    if place is not None and not first:
        refs.pop(0)
    out = refs.pop(0)
    if not last:
        tail = refs.pop(0)
    if first and not last:
        head = refs.pop(0)
    mix, state = refs[:2]
    whole = out
    if place is not None:
        out, sems = refs[2:]
    rows = own.shape[0]
    channels = own.shape[2]
    start = 0 if first else 2 * PAD

    if not first:
        mix[:, : 2 * PAD] = prev_mix[...].astype(jnp.float32)
        state[:, : 2 * PAD] = prev_own[:, prev_own.shape[1] - 2 * PAD :]
    if last and not first:
        mix[:, start + width :] = first_mix[...].astype(jnp.float32)
        state[:, start + width :] = first_own[:, : 2 * PAD]

    band = lax.axis_index("band")
    is_odd = lax.rem(band, 2) == 1
    lat_rows = lat_w[...].astype(jnp.float32)
    lat_tap = [jnp.broadcast_to(lat_rows[k, layer : layer + 1], (PAD, channels)) for k in range(TAPS)]

    def mix_tile(t, carry):
        at = pl.multiple_of(t * PAD, PAD)
        to = pl.multiple_of(start + t * PAD, PAD)
        evens = [even_swap[r, pl.ds(at, PAD)] for r in range(REACH)]
        odds = [odd_swap[r, pl.ds(at, PAD)] for r in range(REACH)]
        above = [jnp.where(is_odd, e, o) for e, o in zip(evens, odds)]
        below = [jnp.where(is_odd, o, e) for e, o in zip(evens, odds)]
        mine = [own[r, pl.ds(at, PAD)] for r in range(rows)]
        strip = [s.astype(jnp.float32) for s in above + mine + below]
        for r in range(rows):
            total = strip[r] * lat_tap[0]
            for k in range(1, TAPS):
                total = total + strip[r + k] * lat_tap[k]
            mix[r, pl.ds(to, PAD)] = total.astype(jnp.bfloat16).astype(jnp.float32)
            state[r, pl.ds(to, PAD)] = mine[r]
        return carry

    lax.fori_loop(0, width // PAD, mix_tile, 0, unroll=2)

    if not last:
        tail[...] = mix[:, start + width - 2 * PAD : start + width].astype(jnp.bfloat16)
    if first and not last:
        head[...] = mix[:, : 2 * PAD].astype(jnp.bfloat16)
    if first and last:
        mix[:, width:] = mix[:, : 2 * PAD]
        state[:, width:] = state[:, : 2 * PAD]

    lon_rows = lon_w[...].astype(jnp.float32)
    lon_tap = [lon_rows[k, layer : layer + 1] for k in range(TAPS)]
    scale = gain[layer : layer + 1]
    made, total = out.shape[1], whole.shape[1]

    def rest(at, tile):
        parts = []
        for r in range(rows):
            lon = mix[r, pl.ds(at + PAD - DLON * REACH, tile)] * lon_tap[0]
            for k in range(1, TAPS):
                lon = lon + mix[r, pl.ds(at + PAD + DLON * (k - REACH), tile)] * lon_tap[k]
            parts.append(lon)
        lon = jnp.concatenate(parts, axis=0)
        mean = jnp.mean(lon, axis=-1, keepdims=True)
        centred = lon - mean
        var = jnp.mean(centred * centred, axis=-1, keepdims=True)
        normed = (centred * lax.rsqrt(var + 1e-06) * scale).astype(jnp.bfloat16)
        hidden = jnp.dot(normed, w_in[layer], preferred_element_type=jnp.float32)
        hidden = gelu(hidden).astype(jnp.bfloat16)
        delta = jnp.dot(hidden, w_out[layer], preferred_element_type=jnp.float32)
        for r in range(rows):
            new = state[r, pl.ds(at + PAD, tile)].astype(jnp.float32) + delta[r * tile : (r + 1) * tile]
            out[r, pl.ds(at, tile)] = new.astype(jnp.bfloat16)

    copies = []
    for at, tile in tiles(made, total, place):
        rest(at, tile)
        if place is not None:
            to = (place + at) % total
            copies.append(
                pltpu.make_async_copy(out.at[:, at : at + tile], whole.at[:, to : to + tile], sems.at[len(copies)])
            )
            copies[-1].start()
    for copy in copies:
        copy.wait()


def tiles(made, total, place):
    edges = set(range(0, made, TILE)) | {made}
    if place is not None and place + made > total:
        edges = set(range(0, total - place, TILE)) | set(range(total - place, made, TILE)) | {made}
    edges = sorted(edges)
    return [(lo, hi - lo) for lo, hi in zip(edges[:-1], edges[1:])]


def layer_chunk(layer, weights, chunk, prev, first_chunk, first, last, place=None, whole=None):
    own = chunk[0]
    rows, width, channels = own.shape
    made = width + (0 if first else PAD) + (0 if last else -PAD) + (PAD if last else 0) - (PAD if first else 0)
    window = made + 2 * PAD
    args = list(weights) + list(chunk)
    if not first:
        args += list(prev)
    if last and not first:
        args += list(first_chunk)
    specs = [pl.BlockSpec(memory_space=pltpu.VMEM)] * len(args)
    strip = jax.ShapeDtypeStruct((rows, 2 * PAD, channels), jnp.bfloat16)
    outs = [jax.ShapeDtypeStruct((rows, made, channels), jnp.bfloat16)]
    out_specs = [pl.BlockSpec(memory_space=pltpu.VMEM)]
    scratch = [
        pltpu.VMEM((rows, window, channels), jnp.float32),
        pltpu.VMEM((rows, window, channels), jnp.bfloat16),
    ]
    aliases = {}
    if place is not None:
        lons = whole if first else whole.shape[1]
        scratch += [pltpu.VMEM(outs[0].shape, jnp.bfloat16), pltpu.SemaphoreType.DMA((len(tiles(made, lons, place)),))]
        outs = [jax.ShapeDtypeStruct((rows, lons, channels), jnp.bfloat16)]
        out_specs = [pl.BlockSpec(memory_space=pltpu.HBM)]
        if not first:
            aliases = {len(args): 0}
            args.append(whole)
            specs += out_specs
    if not last:
        outs.append(strip)
    if first and not last:
        outs.append(strip)
    out_specs += [pl.BlockSpec(memory_space=pltpu.VMEM)] * (len(outs) - 1)
    cells = rows * made
    hidden = weights[3].shape[2]
    return pl.pallas_call(
        functools.partial(chunk_kernel, layer, first, last, width, place),
        out_shape=outs,
        in_specs=specs,
        out_specs=out_specs,
        scratch_shapes=scratch,
        input_output_aliases=aliases,
        compiler_params=pltpu.CompilerParams(vmem_limit_bytes=24 * 2**20),
        cost_estimate=pl.CostEstimate(
            flops=50 * cells * channels * hidden, bytes_accessed=8 * cells * channels, transcendentals=cells * hidden
        ),
    )(*args)


def splits(total):
    first = PAD * ((total // PAD + 2) // 2)
    return [(0, first), (first, total)]


def swaps(bands, start):
    return [pair for b in range(start, bands - 1, 2) for pair in ((b, b + 1), (b + 1, b))]


def member_step(state, weights, bands):
    rows, lons, _ = state.shape
    assert rows == REACH
    even_pairs, odd_pairs = swaps(bands, 0), swaps(bands, 1)
    ranges = splits(lons)
    chunks = [state[:, : ranges[0][1]]]
    for lo, hi in ranges[1:]:
        chunks.append(later_columns(state, lo, hi, chunks[1:][-1:]))
    whole, place = lons, LAYERS * PAD
    for layer in range(LAYERS):
        halos = []
        for own in chunks:
            odd_swap = lax.ppermute(own, "band", odd_pairs)
            even_swap = lax.ppermute(own, "band", even_pairs)
            halos.append((odd_swap, even_swap))
        final = layer == LAYERS - 1
        made, prev, first_chunk = [], None, None
        for c, own in enumerate(chunks):
            first, last = c == 0, c == len(chunks) - 1
            where = (place, whole) if final else ()
            got = layer_chunk(layer, weights, (own,) + halos[c], prev, first_chunk, first, last, *where)
            made.append(got[0])
            if final:
                whole = got[0]
                place += own.shape[1] - (2 * PAD if first else 0)
            if not last:
                prev = (own, got[1])
            if first and not last:
                first_chunk = (own, got[2])
        chunks = made
    return whole


def solution(mesh):
    bands = mesh.shape["band"]

    def shards(fields, lat_taps, lon_taps, gains, w_in, w_out):
        weights = (lat_taps.transpose(1, 0, 2), lon_taps.transpose(1, 0, 2), gains, w_in, w_out)
        return jnp.concatenate([member_step(fields[m], weights, bands)[None] for m in range(fields.shape[0])])

    return jax.shard_map(
        shards,
        mesh=mesh,
        in_specs=(P(("members", "section"), "band", None, None), P(), P(), P(), P(), P()),
        out_specs=P(("members", "section"), "band", None, None),
        check_vma=False,
    )
```

```python
import functools

import jax
import jax.numpy as jnp
from jax import lax
from jax.experimental import pallas as pl
from jax.experimental.pallas import tpu as pltpu
from jax.sharding import PartitionSpec as P

DLON = 3
LAYERS = 2
TAPS = 9
REACH = TAPS // 2
PAD = 16
TILE = 32


def gelu(x):
    return 0.5 * x * (1.0 + lax.erf(x * 0.7071067811865476))


def copy_kernel(lo, state, *refs):
    out = refs[-1]
    out[...] = state[:, lo : lo + out.shape[1]]


def later_columns(state, lo, hi, after):
    rows, _, channels = state.shape
    return pl.pallas_call(
        functools.partial(copy_kernel, lo),
        out_shape=jax.ShapeDtypeStruct((rows, hi - lo, channels), state.dtype),
        in_specs=[pl.BlockSpec(memory_space=pltpu.VMEM)] * (1 + len(after)),
        out_specs=pl.BlockSpec(memory_space=pltpu.VMEM),
        compiler_params=pltpu.CompilerParams(vmem_limit_bytes=16 * 2**20),
        cost_estimate=pl.CostEstimate(flops=2 * 10**9, bytes_accessed=4 * rows * (hi - lo) * channels, transcendentals=0),
    )(state, *after)


def chunk_kernel(layer, first, last, offset, width, prev_end, place, *refs):
    refs = list(refs)
    lat_w, lon_w, gain, w_in, w_out, own, odd_swap, even_swap = refs[:8]
    refs = refs[8:]
    if not first:
        prev_own, prev_mix = refs[:2]
        refs = refs[2:]
    if last and not first:
        first_own, first_mix = refs[:2]
        refs = refs[2:]
    if place is not None and not first:
        refs.pop(0)
    out = refs.pop(0)
    if not last:
        tail = refs.pop(0)
    if first and not last:
        head = refs.pop(0)
    mix, state = refs[:2]
    whole = out
    if place is not None:
        out, sems = refs[2:]
    rows = own.shape[0]
    channels = own.shape[2]
    start = 0 if first else 2 * PAD

    if not first:
        mix[:, : 2 * PAD] = prev_mix[...].astype(jnp.float32)
        state[:, : 2 * PAD] = prev_own[:, prev_end - 2 * PAD : prev_end]
    if last and not first:
        mix[:, start + width :] = first_mix[...].astype(jnp.float32)
        state[:, start + width :] = first_own[:, : 2 * PAD]

    band = lax.axis_index("band")
    is_odd = lax.rem(band, 2) == 1
    lat_rows = lat_w[...].astype(jnp.float32)
    lat_tap = [jnp.broadcast_to(lat_rows[k, layer : layer + 1], (PAD, channels)) for k in range(TAPS)]

    def mix_tile(t, carry):
        at = pl.multiple_of(offset + t * PAD, PAD)
        to = pl.multiple_of(start + t * PAD, PAD)
        evens = [even_swap[r, pl.ds(at, PAD)] for r in range(REACH)]
        odds = [odd_swap[r, pl.ds(at, PAD)] for r in range(REACH)]
        above = [jnp.where(is_odd, e, o) for e, o in zip(evens, odds)]
        below = [jnp.where(is_odd, o, e) for e, o in zip(evens, odds)]
        mine = [own[r, pl.ds(at, PAD)] for r in range(rows)]
        strip = [s.astype(jnp.float32) for s in above + mine + below]
        for r in range(rows):
            total = strip[r] * lat_tap[0]
            for k in range(1, TAPS):
                total = total + strip[r + k] * lat_tap[k]
            mix[r, pl.ds(to, PAD)] = total.astype(jnp.bfloat16).astype(jnp.float32)
            state[r, pl.ds(to, PAD)] = mine[r]
        return carry

    lax.fori_loop(0, width // PAD, mix_tile, 0, unroll=2)

    if not last:
        tail[...] = mix[:, start + width - 2 * PAD : start + width].astype(jnp.bfloat16)
    if first and not last:
        head[...] = mix[:, : 2 * PAD].astype(jnp.bfloat16)
    if first and last:
        mix[:, width:] = mix[:, : 2 * PAD]
        state[:, width:] = state[:, : 2 * PAD]

    lon_rows = lon_w[...].astype(jnp.float32)
    lon_tap = [lon_rows[k, layer : layer + 1] for k in range(TAPS)]
    scale = gain[layer : layer + 1]
    made, total = out.shape[1], whole.shape[1]

    def rest(at, tile):
        parts = []
        for r in range(rows):
            lon = mix[r, pl.ds(at + PAD - DLON * REACH, tile)] * lon_tap[0]
            for k in range(1, TAPS):
                lon = lon + mix[r, pl.ds(at + PAD + DLON * (k - REACH), tile)] * lon_tap[k]
            parts.append(lon)
        lon = jnp.concatenate(parts, axis=0)
        mean = jnp.mean(lon, axis=-1, keepdims=True)
        centred = lon - mean
        var = jnp.mean(centred * centred, axis=-1, keepdims=True)
        normed = (centred * lax.rsqrt(var + 1e-06) * scale).astype(jnp.bfloat16)
        hidden = jnp.dot(normed, w_in[layer], preferred_element_type=jnp.float32)
        hidden = gelu(hidden).astype(jnp.bfloat16)
        delta = jnp.dot(hidden, w_out[layer], preferred_element_type=jnp.float32)
        for r in range(rows):
            new = state[r, pl.ds(at + PAD, tile)].astype(jnp.float32) + delta[r * tile : (r + 1) * tile]
            out[r, pl.ds(at, tile)] = new.astype(jnp.bfloat16)

    copies = []
    for at, tile in tiles(made, total, place):
        rest(at, tile)
        if place is not None:
            to = (place + at) % total
            copies.append(
                pltpu.make_async_copy(out.at[:, at : at + tile], whole.at[:, to : to + tile], sems.at[len(copies)])
            )
            copies[-1].start()
    for copy in copies:
        copy.wait()


def tiles(made, total, place):
    edges = set(range(0, made, TILE)) | {made}
    if place is not None and place + made > total:
        edges = set(range(0, total - place, TILE)) | set(range(total - place, made, TILE)) | {made}
    edges = sorted(edges)
    return [(lo, hi - lo) for lo, hi in zip(edges[:-1], edges[1:])]


def layer_chunk(layer, weights, chunk, offset, width, prev, first_chunk, first, last, place=None, whole=None):
    own = chunk[0]
    rows, _, channels = own.shape
    prev_end = None if first else prev[1]
    made = width + (0 if first else PAD) + (0 if last else -PAD) + (PAD if last else 0) - (PAD if first else 0)
    window = made + 2 * PAD
    args = list(weights) + list(chunk)
    if not first:
        args += [prev[0], prev[2]]
    if last and not first:
        args += list(first_chunk)
    specs = [pl.BlockSpec(memory_space=pltpu.VMEM)] * len(args)
    strip = jax.ShapeDtypeStruct((rows, 2 * PAD, channels), jnp.bfloat16)
    outs = [jax.ShapeDtypeStruct((rows, made, channels), jnp.bfloat16)]
    out_specs = [pl.BlockSpec(memory_space=pltpu.VMEM)]
    scratch = [
        pltpu.VMEM((rows, window, channels), jnp.float32),
        pltpu.VMEM((rows, window, channels), jnp.bfloat16),
    ]
    aliases = {}
    if place is not None:
        lons = whole if first else whole.shape[1]
        scratch += [pltpu.VMEM(outs[0].shape, jnp.bfloat16), pltpu.SemaphoreType.DMA((len(tiles(made, lons, place)),))]
        outs = [jax.ShapeDtypeStruct((rows, lons, channels), jnp.bfloat16)]
        out_specs = [pl.BlockSpec(memory_space=pltpu.HBM)]
        if not first:
            aliases = {len(args): 0}
            args.append(whole)
            specs += out_specs
    if not last:
        outs.append(strip)
    if first and not last:
        outs.append(strip)
    out_specs += [pl.BlockSpec(memory_space=pltpu.VMEM)] * (len(outs) - 1)
    cells = rows * made
    hidden = weights[3].shape[2]
    return pl.pallas_call(
        functools.partial(chunk_kernel, layer, first, last, offset, width, prev_end, place),
        out_shape=outs,
        in_specs=specs,
        out_specs=out_specs,
        scratch_shapes=scratch,
        input_output_aliases=aliases,
        compiler_params=pltpu.CompilerParams(vmem_limit_bytes=24 * 2**20),
        cost_estimate=pl.CostEstimate(
            flops=50 * cells * channels * hidden, bytes_accessed=8 * cells * channels, transcendentals=cells * hidden
        ),
    )(*args)


def splits(total):
    first = PAD * ((total // PAD + 2) // 2)
    return [(0, first), (first, total)]


def swaps(bands, start):
    return [pair for b in range(start, bands - 1, 2) for pair in ((b, b + 1), (b + 1, b))]


def member_step(state, weights, bands):
    rows, lons, _ = state.shape
    assert rows == REACH
    even_pairs, odd_pairs = swaps(bands, 0), swaps(bands, 1)
    ranges = splits(lons)
    chunks = [state[:, : ranges[0][1]]]
    for lo, hi in ranges[1:]:
        chunks.append(later_columns(state, lo, hi, weights))
    whole, place = lons, LAYERS * PAD
    for layer in range(LAYERS):
        halos = []
        for own in chunks:
            odd_swap = lax.ppermute(own, "band", odd_pairs)
            even_swap = lax.ppermute(own, "band", even_pairs)
            halos.append((odd_swap, even_swap))
        final = layer == LAYERS - 1
        pieces = [(c, 0, own.shape[1]) for c, own in enumerate(chunks)]
        if layer == 0:
            c, _, width = pieces.pop()
            cut = 2 * PAD * (width * 3 // (8 * PAD))
            pieces += [(c, 0, cut), (c, cut, width - cut)]
        made, prev, first_chunk = [], None, None
        for p, (c, offset, width) in enumerate(pieces):
            own = chunks[c]
            first, last = p == 0, p == len(pieces) - 1
            where = (place, whole) if final else ()
            got = layer_chunk(
                layer, weights, (own,) + halos[c], offset, width, prev, first_chunk, first, last, *where
            )
            made.append(got[0])
            if final:
                whole = got[0]
                place += width - (2 * PAD if first else 0)
            if not last:
                prev = (own, offset + width, got[1])
            if first and not last:
                first_chunk = (own, got[2])
        chunks = made
    return whole


def solution(mesh):
    bands = mesh.shape["band"]

    def shards(fields, lat_taps, lon_taps, gains, w_in, w_out):
        weights = (lat_taps.transpose(1, 0, 2), lon_taps.transpose(1, 0, 2), gains, w_in, w_out)
        return jnp.concatenate([member_step(fields[m], weights, bands)[None] for m in range(fields.shape[0])])

    return jax.shard_map(
        shards,
        mesh=mesh,
        in_specs=(P(("members", "section"), "band", None, None), P(), P(), P(), P(), P()),
        out_specs=P(("members", "section"), "band", None, None),
        check_vma=False,
    )
```

```python
import functools

import jax
import jax.numpy as jnp
from jax import lax
from jax.experimental import pallas as pl
from jax.experimental.pallas import tpu as pltpu
from jax.sharding import PartitionSpec as P

DLON = 3
LAYERS = 2
TAPS = 9
REACH = TAPS // 2
PAD = 16
TILE = 32


def gelu(x):
    return 0.5 * x * (1.0 + lax.erf(x * 0.7071067811865476))


def copy_kernel(lo, state, *refs):
    out = refs[-1]
    out[...] = state[:, lo : lo + out.shape[1]]


def later_columns(state, lo, hi, after):
    rows, _, channels = state.shape
    return pl.pallas_call(
        functools.partial(copy_kernel, lo),
        out_shape=jax.ShapeDtypeStruct((rows, hi - lo, channels), state.dtype),
        in_specs=[pl.BlockSpec(memory_space=pltpu.VMEM)] * (1 + len(after)),
        out_specs=pl.BlockSpec(memory_space=pltpu.VMEM),
        compiler_params=pltpu.CompilerParams(vmem_limit_bytes=16 * 2**20),
        cost_estimate=pl.CostEstimate(flops=2 * 10**9, bytes_accessed=4 * rows * (hi - lo) * channels, transcendentals=0),
    )(state, *after)


def chunk_kernel(layer, first, last, offset, width, prev_end, place, earlier, *refs):
    refs = list(refs)
    lat_w, lon_w, gain, w_in, w_out, own, odd_swap, even_swap = refs[:8]
    refs = refs[8:]
    if not first:
        prev_own, prev_mix = refs[:2]
        refs = refs[2:]
    if last and not first:
        first_own, first_mix = refs[:2]
        refs = refs[2:]
    results, refs = refs[: len(earlier)], refs[len(earlier) :]
    out = refs.pop(0)
    if not last:
        tail = refs.pop(0)
    if first and not last:
        head = refs.pop(0)
    mix, state = refs[:2]
    whole = out
    copies = []
    if place is not None:
        out, sems = refs[2:]
        for to, result in zip(earlier, results):
            there = whole.at[:, to : to + result.shape[1]]
            copies.append(pltpu.make_async_copy(result, there, sems.at[len(copies)]))
            copies[-1].start()
    rows = own.shape[0]
    channels = own.shape[2]
    start = 0 if first else 2 * PAD

    if not first:
        mix[:, : 2 * PAD] = prev_mix[...].astype(jnp.float32)
        state[:, : 2 * PAD] = prev_own[:, prev_end - 2 * PAD : prev_end]
    if last and not first:
        mix[:, start + width :] = first_mix[...].astype(jnp.float32)
        state[:, start + width :] = first_own[:, : 2 * PAD]

    band = lax.axis_index("band")
    is_odd = lax.rem(band, 2) == 1
    lat_rows = lat_w[...].astype(jnp.float32)
    lat_tap = [jnp.broadcast_to(lat_rows[k, layer : layer + 1], (PAD, channels)) for k in range(TAPS)]

    def mix_tile(t, carry):
        at = pl.multiple_of(offset + t * PAD, PAD)
        to = pl.multiple_of(start + t * PAD, PAD)
        evens = [even_swap[r, pl.ds(at, PAD)] for r in range(REACH)]
        odds = [odd_swap[r, pl.ds(at, PAD)] for r in range(REACH)]
        above = [jnp.where(is_odd, e, o) for e, o in zip(evens, odds)]
        below = [jnp.where(is_odd, o, e) for e, o in zip(evens, odds)]
        mine = [own[r, pl.ds(at, PAD)] for r in range(rows)]
        strip = [s.astype(jnp.float32) for s in above + mine + below]
        for r in range(rows):
            total = strip[r] * lat_tap[0]
            for k in range(1, TAPS):
                total = total + strip[r + k] * lat_tap[k]
            mix[r, pl.ds(to, PAD)] = total.astype(jnp.bfloat16).astype(jnp.float32)
            state[r, pl.ds(to, PAD)] = mine[r]
        return carry

    lax.fori_loop(0, width // PAD, mix_tile, 0, unroll=4)

    if not last:
        tail[...] = mix[:, start + width - 2 * PAD : start + width].astype(jnp.bfloat16)
    if first and not last:
        head[...] = mix[:, : 2 * PAD].astype(jnp.bfloat16)
    if first and last:
        mix[:, width:] = mix[:, : 2 * PAD]
        state[:, width:] = state[:, : 2 * PAD]

    lon_rows = lon_w[...].astype(jnp.float32)
    lon_tap = [lon_rows[k, layer : layer + 1] for k in range(TAPS)]
    scale = gain[layer : layer + 1]
    made, total = out.shape[1], whole.shape[1]

    def rest(at, tile):
        parts = []
        for r in range(rows):
            lon = mix[r, pl.ds(at + PAD - DLON * REACH, tile)] * lon_tap[0]
            for k in range(1, TAPS):
                lon = lon + mix[r, pl.ds(at + PAD + DLON * (k - REACH), tile)] * lon_tap[k]
            parts.append(lon)
        lon = jnp.concatenate(parts, axis=0)
        mean = jnp.mean(lon, axis=-1, keepdims=True)
        centred = lon - mean
        var = jnp.mean(centred * centred, axis=-1, keepdims=True)
        normed = (centred * lax.rsqrt(var + 1e-06) * scale).astype(jnp.bfloat16)
        hidden = jnp.dot(normed, w_in[layer], preferred_element_type=jnp.float32)
        hidden = gelu(hidden).astype(jnp.bfloat16)
        delta = jnp.dot(hidden, w_out[layer], preferred_element_type=jnp.float32)
        for r in range(rows):
            new = state[r, pl.ds(at + PAD, tile)].astype(jnp.float32) + delta[r * tile : (r + 1) * tile]
            out[r, pl.ds(at, tile)] = new.astype(jnp.bfloat16)

    for at, tile in tiles(made, total, place):
        rest(at, tile)
        if place is not None:
            to = (place + at) % total
            copies.append(
                pltpu.make_async_copy(out.at[:, at : at + tile], whole.at[:, to : to + tile], sems.at[len(copies)])
            )
            copies[-1].start()
    for copy in copies:
        copy.wait()


def tiles(made, total, place):
    edges = set(range(0, made, TILE)) | {made}
    if place is not None and place + made > total:
        edges = set(range(0, total - place, TILE)) | set(range(total - place, made, TILE)) | {made}
    edges = sorted(edges)
    return [(lo, hi - lo) for lo, hi in zip(edges[:-1], edges[1:])]


def layer_chunk(layer, weights, chunk, offset, width, prev, first_chunk, first, last, place=None, lons=None, earlier=()):
    own = chunk[0]
    rows, _, channels = own.shape
    prev_end = None if first else prev[1]
    made = width + (0 if first else PAD) + (0 if last else -PAD) + (PAD if last else 0) - (PAD if first else 0)
    window = made + 2 * PAD
    args = list(weights) + list(chunk)
    if not first:
        args += [prev[0], prev[2]]
    if last and not first:
        args += list(first_chunk)
    specs = [pl.BlockSpec(memory_space=pltpu.VMEM)] * len(args)
    strip = jax.ShapeDtypeStruct((rows, 2 * PAD, channels), jnp.bfloat16)
    outs = [jax.ShapeDtypeStruct((rows, made, channels), jnp.bfloat16)]
    out_specs = [pl.BlockSpec(memory_space=pltpu.VMEM)]
    scratch = [
        pltpu.VMEM((rows, window, channels), jnp.float32),
        pltpu.VMEM((rows, window, channels), jnp.bfloat16),
    ]
    if place is not None:
        sems = len(earlier) + len(tiles(made, lons, place))
        scratch += [pltpu.VMEM(outs[0].shape, jnp.bfloat16), pltpu.SemaphoreType.DMA((sems,))]
        outs = [jax.ShapeDtypeStruct((rows, lons, channels), jnp.bfloat16)]
        out_specs = [pl.BlockSpec(memory_space=pltpu.HBM)]
        args += [result for _, result in earlier]
        specs += [pl.BlockSpec(memory_space=pltpu.VMEM)] * len(earlier)
    if not last:
        outs.append(strip)
    if first and not last:
        outs.append(strip)
    out_specs += [pl.BlockSpec(memory_space=pltpu.VMEM)] * (len(outs) - 1)
    cells = rows * made
    hidden = weights[3].shape[2]
    return pl.pallas_call(
        functools.partial(chunk_kernel, layer, first, last, offset, width, prev_end, place, [at for at, _ in earlier]),
        out_shape=outs,
        in_specs=specs,
        out_specs=out_specs,
        scratch_shapes=scratch,
        compiler_params=pltpu.CompilerParams(vmem_limit_bytes=24 * 2**20),
        cost_estimate=pl.CostEstimate(
            flops=50 * cells * channels * hidden, bytes_accessed=8 * cells * channels, transcendentals=cells * hidden
        ),
    )(*args)


def splits(total):
    first = PAD * ((total // PAD + 2) // 2)
    return [(0, first), (first, total)]


def swaps(bands, start):
    return [pair for b in range(start, bands - 1, 2) for pair in ((b, b + 1), (b + 1, b))]


def member_step(state, weights, bands):
    rows, lons, _ = state.shape
    assert rows == REACH
    even_pairs, odd_pairs = swaps(bands, 0), swaps(bands, 1)
    ranges = splits(lons)
    chunks = [state[:, : ranges[0][1]]]
    for lo, hi in ranges[1:]:
        chunks.append(later_columns(state, lo, hi, weights))
    place, earlier = LAYERS * PAD, []
    for layer in range(LAYERS):
        halos = []
        for own in chunks:
            odd_swap = lax.ppermute(own, "band", odd_pairs)
            even_swap = lax.ppermute(own, "band", even_pairs)
            halos.append((odd_swap, even_swap))
        final = layer == LAYERS - 1
        pieces = [(c, 0, own.shape[1]) for c, own in enumerate(chunks)]
        if layer == 0:
            c, _, width = pieces.pop()
            cut = 2 * PAD * (width * 3 // (8 * PAD))
            pieces += [(c, 0, cut), (c, cut, width - cut)]
        made, prev, first_chunk = [], None, None
        for p, (c, offset, width) in enumerate(pieces):
            own = chunks[c]
            first, last = p == 0, p == len(pieces) - 1
            where = (place, lons, earlier) if final and last else ()
            got = layer_chunk(
                layer, weights, (own,) + halos[c], offset, width, prev, first_chunk, first, last, *where
            )
            made.append(got[0])
            if final:
                earlier.append((place, got[0]))
                place += got[0].shape[1]
            if not last:
                prev = (own, offset + width, got[1])
            if first and not last:
                first_chunk = (own, got[2])
        chunks = made
    return chunks[-1]


def solution(mesh):
    bands = mesh.shape["band"]

    def shards(fields, lat_taps, lon_taps, gains, w_in, w_out):
        weights = (lat_taps.transpose(1, 0, 2), lon_taps.transpose(1, 0, 2), gains, w_in, w_out)
        return jnp.concatenate([member_step(fields[m], weights, bands)[None] for m in range(fields.shape[0])])

    return jax.shard_map(
        shards,
        mesh=mesh,
        in_specs=(P(("members", "section"), "band", None, None), P(), P(), P(), P(), P()),
        out_specs=P(("members", "section"), "band", None, None),
        check_vma=False,
    )
```

```python
import functools

import jax
import jax.numpy as jnp
from jax import lax
from jax.experimental import pallas as pl
from jax.experimental.pallas import tpu as pltpu
from jax.sharding import PartitionSpec as P

DLON = 3
LAYERS = 2
TAPS = 9
REACH = TAPS // 2
PAD = 16
TILE = 32


def gelu(x):
    return 0.5 * x * (1.0 + lax.erf(x * 0.7071067811865476))


def copy_kernel(lo, state, *refs):
    out = refs[-1]
    out[...] = state[:, lo : lo + out.shape[1]]


def later_columns(state, lo, hi, after):
    rows, _, channels = state.shape
    return pl.pallas_call(
        functools.partial(copy_kernel, lo),
        out_shape=jax.ShapeDtypeStruct((rows, hi - lo, channels), state.dtype),
        in_specs=[pl.BlockSpec(memory_space=pltpu.VMEM)] * (1 + len(after)),
        out_specs=pl.BlockSpec(memory_space=pltpu.VMEM),
        compiler_params=pltpu.CompilerParams(vmem_limit_bytes=16 * 2**20),
        cost_estimate=pl.CostEstimate(flops=2 * 10**9, bytes_accessed=4 * rows * (hi - lo) * channels, transcendentals=0),
    )(state, *after)


def chunk_kernel(layer, first, last, offset, width, prev_end, place, earlier, *refs):
    refs = list(refs)
    lat_w, lon_w, gain, w_in, w_out, own, even_swap, odd_swap = refs[:8]
    refs = refs[8:]
    if not first:
        prev_own, prev_mix = refs[:2]
        refs = refs[2:]
    if last and not first:
        first_own, first_mix = refs[:2]
        refs = refs[2:]
    results, refs = refs[: len(earlier)], refs[len(earlier) :]
    out = refs.pop(0)
    if not last:
        tail = refs.pop(0)
    if first and not last:
        head = refs.pop(0)
    mix, state = refs[:2]
    whole = out
    copies = []
    if place is not None:
        out, sems = refs[2:]
        for to, result in zip(earlier, results):
            there = whole.at[:, to : to + result.shape[1]]
            copies.append(pltpu.make_async_copy(result, there, sems.at[len(copies)]))
            copies[-1].start()
    rows = own.shape[0]
    channels = own.shape[2]
    start = 0 if first else 2 * PAD

    if not first:
        mix[:, : 2 * PAD] = prev_mix[...].astype(jnp.float32)
        state[:, : 2 * PAD] = prev_own[:, prev_end - 2 * PAD : prev_end]
    if last and not first:
        mix[:, start + width :] = first_mix[...].astype(jnp.float32)
        state[:, start + width :] = first_own[:, : 2 * PAD]

    band = lax.axis_index("band")
    is_odd = lax.rem(band, 2) == 1
    lat_rows = lat_w[...].astype(jnp.float32)
    lat_tap = [jnp.broadcast_to(lat_rows[k, layer : layer + 1], (PAD, channels)) for k in range(TAPS)]

    def mix_tile(t, carry):
        at = pl.multiple_of(offset + t * PAD, PAD)
        to = pl.multiple_of(start + t * PAD, PAD)
        evens = [even_swap[r, pl.ds(at, PAD)] for r in range(REACH)]
        odds = [odd_swap[r, pl.ds(at, PAD)] for r in range(REACH)]
        above = [jnp.where(is_odd, e, o) for e, o in zip(evens, odds)]
        below = [jnp.where(is_odd, o, e) for e, o in zip(evens, odds)]
        mine = [own[r, pl.ds(at, PAD)] for r in range(rows)]
        strip = [s.astype(jnp.float32) for s in above + mine + below]
        for r in range(rows):
            total = strip[r] * lat_tap[0]
            for k in range(1, TAPS):
                total = total + strip[r + k] * lat_tap[k]
            mix[r, pl.ds(to, PAD)] = total.astype(jnp.bfloat16).astype(jnp.float32)
            state[r, pl.ds(to, PAD)] = mine[r]
        return carry

    lax.fori_loop(0, width // PAD, mix_tile, 0, unroll=4)

    if not last:
        tail[...] = mix[:, start + width - 2 * PAD : start + width].astype(jnp.bfloat16)
    if first and not last:
        head[...] = mix[:, : 2 * PAD].astype(jnp.bfloat16)
    if first and last:
        mix[:, width:] = mix[:, : 2 * PAD]
        state[:, width:] = state[:, : 2 * PAD]

    lon_rows = lon_w[...].astype(jnp.float32)
    lon_tap = [lon_rows[k, layer : layer + 1] for k in range(TAPS)]
    scale = gain[layer : layer + 1]
    made, total = out.shape[1], whole.shape[1]

    def rest(at, tile):
        parts = []
        for r in range(rows):
            lon = mix[r, pl.ds(at + PAD - DLON * REACH, tile)] * lon_tap[0]
            for k in range(1, TAPS):
                lon = lon + mix[r, pl.ds(at + PAD + DLON * (k - REACH), tile)] * lon_tap[k]
            parts.append(lon)
        lon = jnp.concatenate(parts, axis=0)
        mean = jnp.mean(lon, axis=-1, keepdims=True)
        centred = lon - mean
        var = jnp.mean(centred * centred, axis=-1, keepdims=True)
        normed = (centred * lax.rsqrt(var + 1e-06) * scale).astype(jnp.bfloat16)
        hidden = jnp.dot(normed, w_in[layer], preferred_element_type=jnp.float32)
        hidden = gelu(hidden).astype(jnp.bfloat16)
        delta = jnp.dot(hidden, w_out[layer], preferred_element_type=jnp.float32)
        for r in range(rows):
            new = state[r, pl.ds(at + PAD, tile)].astype(jnp.float32) + delta[r * tile : (r + 1) * tile]
            out[r, pl.ds(at, tile)] = new.astype(jnp.bfloat16)

    for at, tile in tiles(made, total, place):
        rest(at, tile)
        if place is not None:
            to = (place + at) % total
            copies.append(
                pltpu.make_async_copy(out.at[:, at : at + tile], whole.at[:, to : to + tile], sems.at[len(copies)])
            )
            copies[-1].start()
    for copy in copies:
        copy.wait()


def tiles(made, total, place):
    edges = set(range(0, made, TILE)) | {made}
    if place is not None and place + made > total:
        edges = set(range(0, total - place, TILE)) | set(range(total - place, made, TILE)) | {made}
    edges = sorted(edges)
    return [(lo, hi - lo) for lo, hi in zip(edges[:-1], edges[1:])]


def layer_chunk(layer, weights, chunk, offset, width, prev, first_chunk, first, last, place=None, lons=None, earlier=()):
    own = chunk[0]
    rows, _, channels = own.shape
    prev_end = None if first else prev[1]
    made = width + (0 if first else PAD) + (0 if last else -PAD) + (PAD if last else 0) - (PAD if first else 0)
    window = made + 2 * PAD
    args = list(weights) + list(chunk)
    if not first:
        args += [prev[0], prev[2]]
    if last and not first:
        args += list(first_chunk)
    specs = [pl.BlockSpec(memory_space=pltpu.VMEM)] * len(args)
    strip = jax.ShapeDtypeStruct((rows, 2 * PAD, channels), jnp.bfloat16)
    outs = [jax.ShapeDtypeStruct((rows, made, channels), jnp.bfloat16)]
    out_specs = [pl.BlockSpec(memory_space=pltpu.VMEM)]
    scratch = [
        pltpu.VMEM((rows, window, channels), jnp.float32),
        pltpu.VMEM((rows, window, channels), jnp.bfloat16),
    ]
    if place is not None:
        sems = len(earlier) + len(tiles(made, lons, place))
        scratch += [pltpu.VMEM(outs[0].shape, jnp.bfloat16), pltpu.SemaphoreType.DMA((sems,))]
        outs = [jax.ShapeDtypeStruct((rows, lons, channels), jnp.bfloat16)]
        out_specs = [pl.BlockSpec(memory_space=pltpu.HBM)]
        args += [result for _, result in earlier]
        specs += [pl.BlockSpec(memory_space=pltpu.VMEM)] * len(earlier)
    if not last:
        outs.append(strip)
    if first and not last:
        outs.append(strip)
    out_specs += [pl.BlockSpec(memory_space=pltpu.VMEM)] * (len(outs) - 1)
    cells = rows * made
    hidden = weights[3].shape[2]
    return pl.pallas_call(
        functools.partial(chunk_kernel, layer, first, last, offset, width, prev_end, place, [at for at, _ in earlier]),
        out_shape=outs,
        in_specs=specs,
        out_specs=out_specs,
        scratch_shapes=scratch,
        compiler_params=pltpu.CompilerParams(vmem_limit_bytes=24 * 2**20),
        cost_estimate=pl.CostEstimate(
            flops=50 * cells * channels * hidden, bytes_accessed=8 * cells * channels, transcendentals=cells * hidden
        ),
    )(*args)


def splits(total):
    first = PAD * ((total // PAD + 2) // 2)
    return [(0, first), (first, total)]


def swaps(bands, start):
    return [pair for b in range(start, bands - 1, 2) for pair in ((b, b + 1), (b + 1, b))]


def member_step(state, weights, bands):
    rows, lons, _ = state.shape
    assert rows == REACH
    even_pairs, odd_pairs = swaps(bands, 0), swaps(bands, 1)
    ranges = splits(lons)
    chunks = [state[:, : ranges[0][1]]]
    for lo, hi in ranges[1:]:
        chunks.append(later_columns(state, lo, hi, weights))
    place, earlier = LAYERS * PAD, []
    for layer in range(LAYERS):
        halos = []
        for own in chunks:
            odd_swap = lax.ppermute(own, "band", odd_pairs)
            even_swap = lax.ppermute(own, "band", even_pairs)
            halos.append((even_swap, odd_swap))
        final = layer == LAYERS - 1
        pieces = [(c, 0, own.shape[1]) for c, own in enumerate(chunks)]
        made, prev, first_chunk = [], None, None
        for p, (c, offset, width) in enumerate(pieces):
            own = chunks[c]
            first, last = p == 0, p == len(pieces) - 1
            where = (place, lons, earlier) if final and last else ()
            got = layer_chunk(
                layer, weights, (own,) + halos[c], offset, width, prev, first_chunk, first, last, *where
            )
            made.append(got[0])
            if final:
                earlier.append((place, got[0]))
                place += got[0].shape[1]
            if not last:
                prev = (own, offset + width, got[1])
            if first and not last:
                first_chunk = (own, got[2])
        chunks = made
    return chunks[-1]


def solution(mesh):
    bands = mesh.shape["band"]

    def shards(fields, lat_taps, lon_taps, gains, w_in, w_out):
        weights = (lat_taps.transpose(1, 0, 2), lon_taps.transpose(1, 0, 2), gains, w_in, w_out)
        return jnp.concatenate([member_step(fields[m], weights, bands)[None] for m in range(fields.shape[0])])

    return jax.shard_map(
        shards,
        mesh=mesh,
        in_specs=(P(("members", "section"), "band", None, None), P(), P(), P(), P(), P()),
        out_specs=P(("members", "section"), "band", None, None),
        check_vma=False,
    )
```

```python
import functools

import jax
import jax.numpy as jnp
from jax import lax
from jax.experimental import pallas as pl
from jax.experimental.pallas import tpu as pltpu
from jax.sharding import PartitionSpec as P

DLON = 3
LAYERS = 2
TAPS = 9
REACH = TAPS // 2
PAD = 16
TILE = 32


def gelu(x):
    return 0.5 * x * (1.0 + lax.erf(x * 0.7071067811865476))


def copy_kernel(lo, state, *refs):
    out = refs[-1]
    out[...] = state[:, lo : lo + out.shape[1]]


def later_columns(state, lo, hi, after):
    rows, _, channels = state.shape
    return pl.pallas_call(
        functools.partial(copy_kernel, lo),
        out_shape=jax.ShapeDtypeStruct((rows, hi - lo, channels), state.dtype),
        in_specs=[pl.BlockSpec(memory_space=pltpu.VMEM)] * (1 + len(after)),
        out_specs=pl.BlockSpec(memory_space=pltpu.VMEM),
        compiler_params=pltpu.CompilerParams(vmem_limit_bytes=16 * 2**20),
        cost_estimate=pl.CostEstimate(flops=2 * 10**9, bytes_accessed=4 * rows * (hi - lo) * channels, transcendentals=0),
    )(state, *after)


def chunk_kernel(layer, first, last, offset, width, prev_end, place, earlier, *refs):
    refs = list(refs)
    lat_w, lon_w, gain, w_in, w_out, own, odd_swap, even_swap = refs[:8]
    refs = refs[8:]
    if not first:
        prev_own, prev_mix = refs[:2]
        refs = refs[2:]
    if last and not first:
        first_own, first_mix = refs[:2]
        refs = refs[2:]
    results, refs = refs[: len(earlier)], refs[len(earlier) :]
    out = refs.pop(0)
    if not last:
        tail = refs.pop(0)
    if first and not last:
        head = refs.pop(0)
    mix, state = refs[:2]
    whole = out
    copies = []
    if place is not None:
        out, sems = refs[2:]
        for to, result in zip(earlier, results):
            there = whole.at[:, to : to + result.shape[1]]
            copies.append(pltpu.make_async_copy(result, there, sems.at[len(copies)]))
            copies[-1].start()
    rows = own.shape[0]
    channels = own.shape[2]
    start = 0 if first else 2 * PAD

    if not first:
        mix[:, : 2 * PAD] = prev_mix[...].astype(jnp.float32)
        state[:, : 2 * PAD] = prev_own[:, prev_end - 2 * PAD : prev_end]
    if last and not first:
        mix[:, start + width :] = first_mix[...].astype(jnp.float32)
        state[:, start + width :] = first_own[:, : 2 * PAD]

    band = lax.axis_index("band")
    is_odd = lax.rem(band, 2) == 1
    lat_rows = lat_w[...].astype(jnp.float32)
    lat_tap = [jnp.broadcast_to(lat_rows[k, layer : layer + 1], (PAD, channels)) for k in range(TAPS)]

    def mix_tile(t, carry):
        at = pl.multiple_of(offset + t * PAD, PAD)
        to = pl.multiple_of(start + t * PAD, PAD)
        evens = [even_swap[r, pl.ds(at, PAD)] for r in range(REACH)]
        odds = [odd_swap[r, pl.ds(at, PAD)] for r in range(REACH)]
        above = [jnp.where(is_odd, e, o) for e, o in zip(evens, odds)]
        below = [jnp.where(is_odd, o, e) for e, o in zip(evens, odds)]
        mine = [own[r, pl.ds(at, PAD)] for r in range(rows)]
        strip = [s.astype(jnp.float32) for s in above + mine + below]
        for r in range(rows):
            total = strip[r] * lat_tap[0]
            for k in range(1, TAPS):
                total = total + strip[r + k] * lat_tap[k]
            mix[r, pl.ds(to, PAD)] = total.astype(jnp.bfloat16).astype(jnp.float32)
            state[r, pl.ds(to, PAD)] = mine[r]
        return carry

    lax.fori_loop(0, width // PAD, mix_tile, 0, unroll=4)

    if not last:
        tail[...] = mix[:, start + width - 2 * PAD : start + width].astype(jnp.bfloat16)
    if first and not last:
        head[...] = mix[:, : 2 * PAD].astype(jnp.bfloat16)
    if first and last:
        mix[:, width:] = mix[:, : 2 * PAD]
        state[:, width:] = state[:, : 2 * PAD]

    lon_rows = lon_w[...].astype(jnp.float32)
    lon_tap = [lon_rows[k, layer : layer + 1] for k in range(TAPS)]
    scale = gain[layer : layer + 1]
    made, total = out.shape[1], whole.shape[1]

    def rest(at, tile):
        parts = []
        for r in range(rows):
            lon = mix[r, pl.ds(at + PAD - DLON * REACH, tile)] * lon_tap[0]
            for k in range(1, TAPS):
                lon = lon + mix[r, pl.ds(at + PAD + DLON * (k - REACH), tile)] * lon_tap[k]
            parts.append(lon)
        lon = jnp.concatenate(parts, axis=0)
        mean = jnp.mean(lon, axis=-1, keepdims=True)
        centred = lon - mean
        var = jnp.mean(centred * centred, axis=-1, keepdims=True)
        normed = (centred * lax.rsqrt(var + 1e-06) * scale).astype(jnp.bfloat16)
        hidden = jnp.dot(normed, w_in[layer], preferred_element_type=jnp.float32)
        hidden = gelu(hidden).astype(jnp.bfloat16)
        delta = jnp.dot(hidden, w_out[layer], preferred_element_type=jnp.float32)
        for r in range(rows):
            new = state[r, pl.ds(at + PAD, tile)].astype(jnp.float32) + delta[r * tile : (r + 1) * tile]
            out[r, pl.ds(at, tile)] = new.astype(jnp.bfloat16)

    for at, tile in tiles(made, total, place):
        rest(at, tile)
        if place is not None:
            to = (place + at) % total
            copies.append(
                pltpu.make_async_copy(out.at[:, at : at + tile], whole.at[:, to : to + tile], sems.at[len(copies)])
            )
            copies[-1].start()
    for copy in copies:
        copy.wait()


def tiles(made, total, place):
    edges = set(range(0, made, TILE)) | {made}
    if place is not None and place + made > total:
        edges = set(range(0, total - place, TILE)) | set(range(total - place, made, TILE)) | {made}
    edges = sorted(edges)
    return [(lo, hi - lo) for lo, hi in zip(edges[:-1], edges[1:])]


def layer_chunk(layer, weights, chunk, offset, width, prev, first_chunk, first, last, place=None, lons=None, earlier=()):
    own = chunk[0]
    rows, _, channels = own.shape
    prev_end = None if first else prev[1]
    made = width + (0 if first else PAD) + (0 if last else -PAD) + (PAD if last else 0) - (PAD if first else 0)
    window = made + 2 * PAD
    args = list(weights) + list(chunk)
    if not first:
        args += [prev[0], prev[2]]
    if last and not first:
        args += list(first_chunk)
    specs = [pl.BlockSpec(memory_space=pltpu.VMEM)] * len(args)
    strip = jax.ShapeDtypeStruct((rows, 2 * PAD, channels), jnp.bfloat16)
    outs = [jax.ShapeDtypeStruct((rows, made, channels), jnp.bfloat16)]
    out_specs = [pl.BlockSpec(memory_space=pltpu.VMEM)]
    scratch = [
        pltpu.VMEM((rows, window, channels), jnp.float32),
        pltpu.VMEM((rows, window, channels), jnp.bfloat16),
    ]
    if place is not None:
        sems = len(earlier) + len(tiles(made, lons, place))
        scratch += [pltpu.VMEM(outs[0].shape, jnp.bfloat16), pltpu.SemaphoreType.DMA((sems,))]
        outs = [jax.ShapeDtypeStruct((rows, lons, channels), jnp.bfloat16)]
        out_specs = [pl.BlockSpec(memory_space=pltpu.HBM)]
        args += [result for _, result in earlier]
        specs += [pl.BlockSpec(memory_space=pltpu.VMEM)] * len(earlier)
    if not last:
        outs.append(strip)
    if first and not last:
        outs.append(strip)
    out_specs += [pl.BlockSpec(memory_space=pltpu.VMEM)] * (len(outs) - 1)
    cells = rows * made
    hidden = weights[3].shape[2]
    return pl.pallas_call(
        functools.partial(chunk_kernel, layer, first, last, offset, width, prev_end, place, [at for at, _ in earlier]),
        out_shape=outs,
        in_specs=specs,
        out_specs=out_specs,
        scratch_shapes=scratch,
        compiler_params=pltpu.CompilerParams(vmem_limit_bytes=24 * 2**20),
        cost_estimate=pl.CostEstimate(
            flops=50 * cells * channels * hidden, bytes_accessed=8 * cells * channels, transcendentals=cells * hidden
        ),
    )(*args)


def splits(total):
    first = PAD * ((total // PAD + 2) // 2)
    return [(0, first), (first, total)]


def swaps(bands, start):
    return [pair for b in range(start, bands - 1, 2) for pair in ((b, b + 1), (b + 1, b))]


def member_step(state, weights, bands):
    rows, lons, _ = state.shape
    assert rows == REACH
    even_pairs, odd_pairs = swaps(bands, 0), swaps(bands, 1)
    ranges = splits(lons)
    chunks = [state[:, : ranges[0][1]]]
    for lo, hi in ranges[1:]:
        chunks.append(later_columns(state, lo, hi, weights))
    place, earlier = LAYERS * PAD, []
    for layer in range(LAYERS):
        halos = []
        for own in chunks:
            odd_swap = lax.ppermute(own, "band", odd_pairs)
            even_swap = lax.ppermute(own, "band", even_pairs)
            halos.append((odd_swap, even_swap))
        final = layer == LAYERS - 1
        pieces = [(c, 0, own.shape[1]) for c, own in enumerate(chunks)]
        if layer == 0:
            c, _, width = pieces.pop()
            cut = 2 * PAD * (5 * width // (12 * PAD))
            pieces += [(c, 0, cut), (c, cut, width - cut)]
        made, prev, first_chunk = [], None, None
        for p, (c, offset, width) in enumerate(pieces):
            own = chunks[c]
            first, last = p == 0, p == len(pieces) - 1
            where = (place, lons, earlier) if final and last else ()
            got = layer_chunk(
                layer, weights, (own,) + halos[c], offset, width, prev, first_chunk, first, last, *where
            )
            made.append(got[0])
            if final:
                earlier.append((place, got[0]))
                place += got[0].shape[1]
            if not last:
                prev = (own, offset + width, got[1])
            if first and not last:
                first_chunk = (own, got[2])
        chunks = made
    return chunks[-1]


def solution(mesh):
    bands = mesh.shape["band"]

    def shards(fields, lat_taps, lon_taps, gains, w_in, w_out):
        weights = (lat_taps.transpose(1, 0, 2), lon_taps.transpose(1, 0, 2), gains, w_in, w_out)
        return jnp.concatenate([member_step(fields[m], weights, bands)[None] for m in range(fields.shape[0])])

    return jax.shard_map(
        shards,
        mesh=mesh,
        in_specs=(P(("members", "section"), "band", None, None), P(), P(), P(), P(), P()),
        out_specs=P(("members", "section"), "band", None, None),
        check_vma=False,
    )
```

```python
import functools

import jax
import jax.numpy as jnp
from jax import lax
from jax.experimental import pallas as pl
from jax.experimental.pallas import tpu as pltpu
from jax.sharding import PartitionSpec as P

DLON = 3
LAYERS = 2
TAPS = 9
REACH = TAPS // 2
PAD = 16
TILE = 32


def twice_gelu(x):
    return x + x * lax.erf(x * 0.7071067811865476)


def copy_kernel(lo, state, *refs):
    out = refs[-1]
    out[...] = state[:, lo : lo + out.shape[1]]


def later_columns(state, lo, hi, after):
    rows, _, channels = state.shape
    return pl.pallas_call(
        functools.partial(copy_kernel, lo),
        out_shape=jax.ShapeDtypeStruct((rows, hi - lo, channels), state.dtype),
        in_specs=[pl.BlockSpec(memory_space=pltpu.VMEM)] * (1 + len(after)),
        out_specs=pl.BlockSpec(memory_space=pltpu.VMEM),
        compiler_params=pltpu.CompilerParams(vmem_limit_bytes=16 * 2**20),
        cost_estimate=pl.CostEstimate(flops=2 * 10**9, bytes_accessed=4 * rows * (hi - lo) * channels, transcendentals=0),
    )(state, *after)


def chunk_kernel(layer, first, last, offset, width, prev_end, place, earlier, *refs):
    refs = list(refs)
    lat_w, lon_w, gain, w_in, w_out, own, odd_swap, even_swap = refs[:8]
    refs = refs[8:]
    if not first:
        prev_own, prev_mix = refs[:2]
        refs = refs[2:]
    if last and not first:
        first_own, first_mix = refs[:2]
        refs = refs[2:]
    results, refs = refs[: len(earlier)], refs[len(earlier) :]
    out = refs.pop(0)
    if not last:
        tail = refs.pop(0)
    if first and not last:
        head = refs.pop(0)
    mix, state = refs[:2]
    whole = out
    copies = []
    if place is not None:
        out, sems = refs[2:]
        for to, result in zip(earlier, results):
            there = whole.at[:, to : to + result.shape[1]]
            copies.append(pltpu.make_async_copy(result, there, sems.at[len(copies)]))
            copies[-1].start()
    rows = own.shape[0]
    channels = own.shape[2]
    start = 0 if first else 2 * PAD

    if not first:
        mix[:, : 2 * PAD] = prev_mix[...].astype(jnp.float32)
        state[:, : 2 * PAD] = prev_own[:, prev_end - 2 * PAD : prev_end]
    if last and not first:
        mix[:, start + width :] = first_mix[...].astype(jnp.float32)
        state[:, start + width :] = first_own[:, : 2 * PAD]

    band = lax.axis_index("band")
    is_odd = lax.rem(band, 2) == 1
    lat_rows = lat_w[...].astype(jnp.float32)
    lat_tap = [jnp.broadcast_to(lat_rows[k, layer : layer + 1], (PAD, channels)) for k in range(TAPS)]

    def mix_tile(t, carry):
        at = pl.multiple_of(offset + t * PAD, PAD)
        to = pl.multiple_of(start + t * PAD, PAD)
        evens = [even_swap[r, pl.ds(at, PAD)] for r in range(REACH)]
        odds = [odd_swap[r, pl.ds(at, PAD)] for r in range(REACH)]
        above = [jnp.where(is_odd, e, o) for e, o in zip(evens, odds)]
        below = [jnp.where(is_odd, o, e) for e, o in zip(evens, odds)]
        mine = [own[r, pl.ds(at, PAD)] for r in range(rows)]
        strip = [s.astype(jnp.float32) for s in above + mine + below]
        for r in range(rows):
            total = strip[r] * lat_tap[0]
            for k in range(1, TAPS):
                total = total + strip[r + k] * lat_tap[k]
            mix[r, pl.ds(to, PAD)] = total.astype(jnp.bfloat16).astype(jnp.float32)
            state[r, pl.ds(to, PAD)] = mine[r]
        return carry

    lax.fori_loop(0, width // PAD, mix_tile, 0, unroll=4)

    if not last:
        tail[...] = mix[:, start + width - 2 * PAD : start + width].astype(jnp.bfloat16)
    if first and not last:
        head[...] = mix[:, : 2 * PAD].astype(jnp.bfloat16)
    if first and last:
        mix[:, width:] = mix[:, : 2 * PAD]
        state[:, width:] = state[:, : 2 * PAD]

    lon_rows = lon_w[...].astype(jnp.float32)
    lon_tap = [lon_rows[k, layer : layer + 1] for k in range(TAPS)]
    scale = gain[layer : layer + 1]
    made, total = out.shape[1], whole.shape[1]

    def rest(at, tile):
        parts = []
        for r in range(rows):
            lon = mix[r, pl.ds(at + PAD - DLON * REACH, tile)] * lon_tap[0]
            for k in range(1, TAPS):
                lon = lon + mix[r, pl.ds(at + PAD + DLON * (k - REACH), tile)] * lon_tap[k]
            parts.append(lon)
        lon = jnp.concatenate(parts, axis=0)
        mean = jnp.mean(lon, axis=-1, keepdims=True)
        centred = lon - mean
        var = jnp.mean(centred * centred, axis=-1, keepdims=True)
        normed = (centred * lax.rsqrt(var + 1e-06) * scale).astype(jnp.bfloat16)
        hidden = jnp.dot(normed, w_in[layer], preferred_element_type=jnp.float32)
        hidden = twice_gelu(hidden).astype(jnp.bfloat16)
        delta = jnp.dot(hidden, w_out[layer], preferred_element_type=jnp.float32)
        for r in range(rows):
            new = state[r, pl.ds(at + PAD, tile)].astype(jnp.float32) + 0.5 * delta[r * tile : (r + 1) * tile]
            out[r, pl.ds(at, tile)] = new.astype(jnp.bfloat16)

    for at, tile in tiles(made, total, place):
        rest(at, tile)
        if place is not None:
            to = (place + at) % total
            copies.append(
                pltpu.make_async_copy(out.at[:, at : at + tile], whole.at[:, to : to + tile], sems.at[len(copies)])
            )
            copies[-1].start()
    for copy in copies:
        copy.wait()


def tiles(made, total, place):
    edges = set(range(0, made, TILE)) | {made}
    if place is not None and place + made > total:
        edges = set(range(0, total - place, TILE)) | set(range(total - place, made, TILE)) | {made}
    edges = sorted(edges)
    return [(lo, hi - lo) for lo, hi in zip(edges[:-1], edges[1:])]


def layer_chunk(layer, weights, chunk, offset, width, prev, first_chunk, first, last, place=None, lons=None, earlier=()):
    own = chunk[0]
    rows, _, channels = own.shape
    prev_end = None if first else prev[1]
    made = width + (0 if first else PAD) + (0 if last else -PAD) + (PAD if last else 0) - (PAD if first else 0)
    window = made + 2 * PAD
    args = list(weights) + list(chunk)
    if not first:
        args += [prev[0], prev[2]]
    if last and not first:
        args += list(first_chunk)
    specs = [pl.BlockSpec(memory_space=pltpu.VMEM)] * len(args)
    strip = jax.ShapeDtypeStruct((rows, 2 * PAD, channels), jnp.bfloat16)
    outs = [jax.ShapeDtypeStruct((rows, made, channels), jnp.bfloat16)]
    out_specs = [pl.BlockSpec(memory_space=pltpu.VMEM)]
    scratch = [
        pltpu.VMEM((rows, window, channels), jnp.float32),
        pltpu.VMEM((rows, window, channels), jnp.bfloat16),
    ]
    if place is not None:
        sems = len(earlier) + len(tiles(made, lons, place))
        scratch += [pltpu.VMEM(outs[0].shape, jnp.bfloat16), pltpu.SemaphoreType.DMA((sems,))]
        outs = [jax.ShapeDtypeStruct((rows, lons, channels), jnp.bfloat16)]
        out_specs = [pl.BlockSpec(memory_space=pltpu.HBM)]
        args += [result for _, result in earlier]
        specs += [pl.BlockSpec(memory_space=pltpu.VMEM)] * len(earlier)
    if not last:
        outs.append(strip)
    if first and not last:
        outs.append(strip)
    out_specs += [pl.BlockSpec(memory_space=pltpu.VMEM)] * (len(outs) - 1)
    cells = rows * made
    hidden = weights[3].shape[2]
    return pl.pallas_call(
        functools.partial(chunk_kernel, layer, first, last, offset, width, prev_end, place, [at for at, _ in earlier]),
        out_shape=outs,
        in_specs=specs,
        out_specs=out_specs,
        scratch_shapes=scratch,
        compiler_params=pltpu.CompilerParams(vmem_limit_bytes=24 * 2**20),
        cost_estimate=pl.CostEstimate(
            flops=50 * cells * channels * hidden, bytes_accessed=8 * cells * channels, transcendentals=cells * hidden
        ),
    )(*args)


def splits(total):
    first = PAD * ((total // PAD + 2) // 2)
    return [(0, first), (first, total)]


def swaps(bands, start):
    return [pair for b in range(start, bands - 1, 2) for pair in ((b, b + 1), (b + 1, b))]


def member_step(state, weights, bands):
    rows, lons, _ = state.shape
    assert rows == REACH
    even_pairs, odd_pairs = swaps(bands, 0), swaps(bands, 1)
    ranges = splits(lons)
    chunks = [state[:, : ranges[0][1]]]
    for lo, hi in ranges[1:]:
        chunks.append(later_columns(state, lo, hi, weights))
    place, earlier = LAYERS * PAD, []
    for layer in range(LAYERS):
        halos = []
        for own in chunks:
            odd_swap = lax.ppermute(own, "band", odd_pairs)
            even_swap = lax.ppermute(own, "band", even_pairs)
            halos.append((odd_swap, even_swap))
        final = layer == LAYERS - 1
        pieces = [(c, 0, own.shape[1]) for c, own in enumerate(chunks)]
        if layer == 0:
            c, _, width = pieces.pop()
            cut = 2 * PAD * (5 * width // (12 * PAD))
            pieces += [(c, 0, cut), (c, cut, width - cut)]
        made, prev, first_chunk = [], None, None
        for p, (c, offset, width) in enumerate(pieces):
            own = chunks[c]
            first, last = p == 0, p == len(pieces) - 1
            where = (place, lons, earlier) if final and last else ()
            got = layer_chunk(
                layer, weights, (own,) + halos[c], offset, width, prev, first_chunk, first, last, *where
            )
            made.append(got[0])
            if final:
                earlier.append((place, got[0]))
                place += got[0].shape[1]
            if not last:
                prev = (own, offset + width, got[1])
            if first and not last:
                first_chunk = (own, got[2])
        chunks = made
    return chunks[-1]


def solution(mesh):
    bands = mesh.shape["band"]

    def shards(fields, lat_taps, lon_taps, gains, w_in, w_out):
        weights = (lat_taps.transpose(1, 0, 2), lon_taps.transpose(1, 0, 2), gains, w_in, w_out)
        return jnp.concatenate([member_step(fields[m], weights, bands)[None] for m in range(fields.shape[0])])

    return jax.shard_map(
        shards,
        mesh=mesh,
        in_specs=(P(("members", "section"), "band", None, None), P(), P(), P(), P(), P()),
        out_specs=P(("members", "section"), "band", None, None),
        check_vma=False,
    )
```

```python
import functools

import jax
import jax.numpy as jnp
from jax import lax
from jax.experimental import pallas as pl
from jax.experimental.pallas import tpu as pltpu
from jax.sharding import PartitionSpec as P

DLON = 3
LAYERS = 2
TAPS = 9
REACH = TAPS // 2
PAD = 16
TILE = 32


def gelu(x):
    return 0.5 * x * (1.0 + lax.erf(x * 0.7071067811865476))


def copy_kernel(lo, state, *refs):
    out = refs[-1]
    out[...] = state[:, lo : lo + out.shape[1]]


def later_columns(state, lo, hi, after):
    rows, _, channels = state.shape
    return pl.pallas_call(
        functools.partial(copy_kernel, lo),
        out_shape=jax.ShapeDtypeStruct((rows, hi - lo, channels), state.dtype),
        in_specs=[pl.BlockSpec(memory_space=pltpu.VMEM)] * (1 + len(after)),
        out_specs=pl.BlockSpec(memory_space=pltpu.VMEM),
        compiler_params=pltpu.CompilerParams(vmem_limit_bytes=16 * 2**20),
        cost_estimate=pl.CostEstimate(flops=2 * 10**9, bytes_accessed=4 * rows * (hi - lo) * channels, transcendentals=0),
    )(state, *after)


def chunk_kernel(layer, first, last, offset, width, prev_end, place, earlier, *refs):
    refs = list(refs)
    lat_w, lon_w, gain, w_in, w_out, own, odd_swap, even_swap = refs[:8]
    refs = refs[8:]
    if not first:
        prev_own, prev_mix = refs[:2]
        refs = refs[2:]
    if last and not first:
        first_own, first_mix = refs[:2]
        refs = refs[2:]
    results, refs = refs[: len(earlier)], refs[len(earlier) :]
    out = refs.pop(0)
    if not last:
        tail = refs.pop(0)
    if first and not last:
        head = refs.pop(0)
    mix, state = refs[:2]
    whole = out
    copies = []
    if place is not None:
        out, sems = refs[2:]
        for to, result in zip(earlier, results):
            there = whole.at[:, to : to + result.shape[1]]
            copies.append(pltpu.make_async_copy(result, there, sems.at[len(copies)]))
            copies[-1].start()
    rows = own.shape[0]
    channels = own.shape[2]
    start = 0 if first else 2 * PAD

    if not first:
        mix[:, : 2 * PAD] = prev_mix[...].astype(jnp.float32)
        state[:, : 2 * PAD] = prev_own[:, prev_end - 2 * PAD : prev_end]
    if last and not first:
        mix[:, start + width :] = first_mix[...].astype(jnp.float32)
        state[:, start + width :] = first_own[:, : 2 * PAD]

    band = lax.axis_index("band")
    is_odd = lax.rem(band, 2) == 1
    lat_rows = lat_w[...].astype(jnp.float32)
    lat_tap = [jnp.broadcast_to(lat_rows[k, layer : layer + 1], (PAD, channels)) for k in range(TAPS)]

    def mix_tile(t, carry):
        at = pl.multiple_of(offset + t * PAD, PAD)
        to = pl.multiple_of(start + t * PAD, PAD)
        evens = [even_swap[r, pl.ds(at, PAD)] for r in range(REACH)]
        odds = [odd_swap[r, pl.ds(at, PAD)] for r in range(REACH)]
        above = [jnp.where(is_odd, e, o) for e, o in zip(evens, odds)]
        below = [jnp.where(is_odd, o, e) for e, o in zip(evens, odds)]
        mine = [own[r, pl.ds(at, PAD)] for r in range(rows)]
        strip = [s.astype(jnp.float32) for s in above + mine + below]
        for r in range(rows):
            total = strip[r] * lat_tap[0]
            for k in range(1, TAPS):
                total = total + strip[r + k] * lat_tap[k]
            mix[r, pl.ds(to, PAD)] = total.astype(jnp.bfloat16).astype(jnp.float32)
            state[r, pl.ds(to, PAD)] = mine[r]
        return carry

    lax.fori_loop(0, width // PAD, mix_tile, 0, unroll=4)

    if not last:
        tail[...] = mix[:, start + width - 2 * PAD : start + width].astype(jnp.bfloat16)
    if first and not last:
        head[...] = mix[:, : 2 * PAD].astype(jnp.bfloat16)
    if first and last:
        mix[:, width:] = mix[:, : 2 * PAD]
        state[:, width:] = state[:, : 2 * PAD]

    lon_rows = lon_w[...].astype(jnp.float32)
    lon_tap = [lon_rows[k, layer : layer + 1] for k in range(TAPS)]
    scale = gain[layer : layer + 1]
    made, total = out.shape[1], whole.shape[1]

    def rest(at, tile):
        parts = []
        for r in range(rows):
            lon = mix[r, pl.ds(at + PAD - DLON * REACH, tile)] * lon_tap[0]
            for k in range(1, TAPS):
                lon = lon + mix[r, pl.ds(at + PAD + DLON * (k - REACH), tile)] * lon_tap[k]
            parts.append(lon)
        lon = jnp.concatenate(parts, axis=0)
        mean = jnp.mean(lon, axis=-1, keepdims=True)
        centred = lon - mean
        var = jnp.mean(centred * centred, axis=-1, keepdims=True)
        normed = (centred * lax.rsqrt(var + 1e-06) * scale).astype(jnp.bfloat16)
        hidden = jnp.dot(normed, w_in[layer], preferred_element_type=jnp.float32)
        hidden = gelu(hidden).astype(jnp.bfloat16)
        delta = jnp.dot(hidden, w_out[layer], preferred_element_type=jnp.float32)
        for r in range(rows):
            new = state[r, pl.ds(at + PAD, tile)].astype(jnp.float32) + delta[r * tile : (r + 1) * tile]
            out[r, pl.ds(at, tile)] = new.astype(jnp.bfloat16)

    for at, tile in tiles(made, total, place):
        rest(at, tile)
        if place is not None:
            to = (place + at) % total
            copies.append(
                pltpu.make_async_copy(out.at[:, at : at + tile], whole.at[:, to : to + tile], sems.at[len(copies)])
            )
            copies[-1].start()
    for copy in copies:
        copy.wait()


def tiles(made, total, place):
    edges = set(range(0, made, TILE)) | {made}
    if place is not None and place + made > total:
        edges = set(range(0, total - place, TILE)) | set(range(total - place, made, TILE)) | {made}
    edges = sorted(edges)
    return [(lo, hi - lo) for lo, hi in zip(edges[:-1], edges[1:])]


def layer_chunk(layer, weights, chunk, offset, width, prev, first_chunk, first, last, place=None, lons=None, earlier=()):
    own = chunk[0]
    rows, _, channels = own.shape
    prev_end = None if first else prev[1]
    made = width + (0 if first else PAD) + (0 if last else -PAD) + (PAD if last else 0) - (PAD if first else 0)
    window = made + 2 * PAD
    args = list(weights) + list(chunk)
    if not first:
        args += [prev[0], prev[2]]
    if last and not first:
        args += list(first_chunk)
    specs = [pl.BlockSpec(memory_space=pltpu.VMEM)] * len(args)
    strip = jax.ShapeDtypeStruct((rows, 2 * PAD, channels), jnp.bfloat16)
    outs = [jax.ShapeDtypeStruct((rows, made, channels), jnp.bfloat16)]
    out_specs = [pl.BlockSpec(memory_space=pltpu.VMEM)]
    scratch = [
        pltpu.VMEM((rows, window, channels), jnp.float32),
        pltpu.VMEM((rows, window, channels), jnp.bfloat16),
    ]
    if place is not None:
        sems = len(earlier) + len(tiles(made, lons, place))
        scratch += [pltpu.VMEM(outs[0].shape, jnp.bfloat16), pltpu.SemaphoreType.DMA((sems,))]
        outs = [jax.ShapeDtypeStruct((rows, lons, channels), jnp.bfloat16)]
        out_specs = [pl.BlockSpec(memory_space=pltpu.HBM)]
        args += [result for _, result in earlier]
        specs += [pl.BlockSpec(memory_space=pltpu.VMEM)] * len(earlier)
    if not last:
        outs.append(strip)
    if first and not last:
        outs.append(strip)
    out_specs += [pl.BlockSpec(memory_space=pltpu.VMEM)] * (len(outs) - 1)
    cells = rows * made
    hidden = weights[3].shape[2]
    return pl.pallas_call(
        functools.partial(chunk_kernel, layer, first, last, offset, width, prev_end, place, [at for at, _ in earlier]),
        out_shape=outs,
        in_specs=specs,
        out_specs=out_specs,
        scratch_shapes=scratch,
        compiler_params=pltpu.CompilerParams(vmem_limit_bytes=24 * 2**20),
        cost_estimate=pl.CostEstimate(
            flops=50 * cells * channels * hidden, bytes_accessed=8 * cells * channels, transcendentals=cells * hidden
        ),
    )(*args)


def splits(total):
    first = PAD * ((total // PAD + 2) // 2)
    return [(0, first), (first, total)]


def swaps(bands, start):
    return [pair for b in range(start, bands - 1, 2) for pair in ((b, b + 1), (b + 1, b))]


def member_step(state, weights, bands):
    rows, lons, _ = state.shape
    assert rows == REACH
    even_pairs, odd_pairs = swaps(bands, 0), swaps(bands, 1)
    ranges = splits(lons)
    chunks = [state[:, : ranges[0][1]]]
    for lo, hi in ranges[1:]:
        chunks.append(later_columns(state, lo, hi, weights[:4]))
    place, earlier = LAYERS * PAD, []
    for layer in range(LAYERS):
        halos = []
        for own in chunks:
            odd_swap = lax.ppermute(own, "band", odd_pairs)
            even_swap = lax.ppermute(own, "band", even_pairs)
            halos.append((odd_swap, even_swap))
        final = layer == LAYERS - 1
        pieces = [(c, 0, own.shape[1]) for c, own in enumerate(chunks)]
        if layer == 0:
            c, _, width = pieces.pop()
            cut = 2 * PAD * (5 * width // (12 * PAD))
            pieces += [(c, 0, cut), (c, cut, width - cut)]
        made, prev, first_chunk = [], None, None
        for p, (c, offset, width) in enumerate(pieces):
            own = chunks[c]
            first, last = p == 0, p == len(pieces) - 1
            where = (place, lons, earlier) if final and last else ()
            got = layer_chunk(
                layer, weights, (own,) + halos[c], offset, width, prev, first_chunk, first, last, *where
            )
            made.append(got[0])
            if final:
                earlier.append((place, got[0]))
                place += got[0].shape[1]
            if not last:
                prev = (own, offset + width, got[1])
            if first and not last:
                first_chunk = (own, got[2])
        chunks = made
    return chunks[-1]


def solution(mesh):
    bands = mesh.shape["band"]

    def shards(fields, lat_taps, lon_taps, gains, w_in, w_out):
        weights = (lat_taps.transpose(1, 0, 2), lon_taps.transpose(1, 0, 2), gains, w_in, w_out)
        return jnp.concatenate([member_step(fields[m], weights, bands)[None] for m in range(fields.shape[0])])

    return jax.shard_map(
        shards,
        mesh=mesh,
        in_specs=(P(("members", "section"), "band", None, None), P(), P(), P(), P(), P()),
        out_specs=P(("members", "section"), "band", None, None),
        check_vma=False,
    )
```
